512 devices in a mesh: depth: 4 (over y), seq: 32 (over z, x_lo), rep: 4 (over x_hi, core).
Axes of the slice: x: 4 (x_hi: 2, x_lo: 2; x = x_hi * 2 + x_lo), y: 4, z: 16, core: 2. Of those that a mesh axis runs over, the one named last changes fastest.
Arguments:
- read_feats: bfloat16 [4, 2048, 128, 512], P('rep', 'seq', 'depth'), may hold values from -96 to 96
- base_codes: int32 [4, 2048, 128], P('rep', 'seq', 'depth'), may hold values from 0 to 7
- qual_codes: int32 [4, 2048, 128], P('rep', 'seq', 'depth'), may hold values from 0 to 93
- depth_counts: int32 [4, 2048], P('rep', 'seq'), may hold values from 4 to 128, as said below
- base_table: bfloat16 [8, 512], replicated, may hold values from -3 to 3
- qual_table: bfloat16 [94, 512], replicated, may hold values from -3 to 3
- value_weight: bfloat16 [1024, 512], replicated, may hold values from -0.25 to 0.25
- score_weight: bfloat16 [512, 8], replicated, may hold values from -1 to 1
- conv_weight: bfloat16 [1024, 5, 512], P('depth'), may hold values from -0.078125 to 0.078125
- cotangent: bfloat16 [4, 2048, 512], P('rep', 'seq'), may hold values from -0.15625 to 0.15625
Outputs:
- value_weight_grad: float32 [1024, 512], P(('depth', 'seq', 'rep'))
- score_weight_grad: float32 [512, 8], replicated
- conv_weight_grad: float32 [1024, 5, 512], P(('depth', 'seq'), None, 'rep')
The draws below stay inside these ranges and needn't reach their ends.
Inputs may be any that keep to these rules, and one draw needn't show every extreme that they name: `depth_counts`: reads at or beyond the count are padding; some positions of every window hold 128 live reads.
All inputs are finite; a program needn't handle non-finite values.
Results may differ from the reference program's by a relative error of at most 0.035.
Values may be sent and summed in bfloat16 or wider, within the bound.
No kernel may reach another device: no remote copies, remote signals or barrier semaphores. Data moves between devices by JAX's collectives and lax.ppermute only.
A program may use at most 128 MiB of HBM per device.

```python
import jax
import jax.numpy as jnp
from jax import lax

C = 512
HEADS = 8
HEAD_SIZE = 128
HD = 1024
CO = 512
KERNEL = 5
READS = 128
BASES = 8
QUALS = 94
P_DEV = 64
POS = 2048
WINDOWS = 4


def score_direction(key):
    base = jnp.clip(jax.random.normal(key, (C, HEADS), jnp.float32), -6.0, 6.0) * C ** (-0.5)
    return jnp.clip(base, -1.0, 1.0)


def draw_score_weight(key, part):
    weights = score_direction(key)
    return weights.astype(jnp.bfloat16)


def draw_read_feats(key, part):
    key = jax.random.fold_in(key, 7)
    noise_key = jax.random.fold_in(key, 0)
    noise = jnp.clip(jax.random.normal(noise_key, (WINDOWS, POS, READS, C), jnp.float32), -6.0, 6.0)
    return jnp.clip(noise, -96.0, 96.0).astype(jnp.bfloat16)


def draw_depth_counts(key, part):
    key = jax.random.fold_in(key, 5)
    counts = jax.random.randint(key, (WINDOWS, POS), 4, READS + 1, jnp.int32)
    position = jnp.arange(POS, dtype=jnp.int32)[None, :]
    counts = jnp.where(position % 8 == 5, READS, counts)
    return jnp.where(position % 8 == 2, 4, counts).astype(jnp.int32)


def touch_ends(values, stream_key, low, high):
    index_at = [jax.random.randint(jax.random.fold_in(stream_key, axis), (), 0, length) for axis, length in enumerate(values.shape)]
    longest = values.shape.index(max(values.shape))
    next_to = index_at[:longest] + [(index_at[longest] + 1) % values.shape[longest]] + index_at[longest + 1:]
    return values.at[tuple(index_at)].set(low).at[tuple(next_to)].set(high)


def block_levels(stream_key, shape, cuts, low, largest):
    def one(dim, blocks):
        draws = jax.random.uniform(jax.random.fold_in(jax.random.fold_in(stream_key, 6), dim), (blocks,), jnp.float32, low / len(cuts), largest / len(cuts))
        return jnp.repeat(jnp.exp(draws), shape[dim] // blocks).reshape((-1,) + (1,) * (len(shape) - dim - 1))

    loudness = one(*cuts[0])
    for cut in cuts[1:]:
        loudness = loudness * one(*cut)
    return loudness


def normal_values(own_key, shape, deviation, reach, cuts=(), kind=jnp.bfloat16):
    values = deviation * jax.random.normal(own_key, shape, jnp.float32)
    if cuts:
        values = values * block_levels(own_key, shape, cuts, -0.22, 0.18)
    return jnp.clip(values, -reach, reach).astype(kind)


def setup_inputs(seed: int = 0) -> dict:
    keys = jax.random.split(jax.random.key(seed), 11)
    return {
        "read_feats": draw_read_feats(jax.random.fold_in(keys[10], 71), 0),
        "base_codes": touch_ends(jax.random.randint(keys[1], (WINDOWS, POS, READS), 0, BASES), jax.random.fold_in(keys[1], 1), 0, BASES - 1).astype(jnp.int32),
        "qual_codes": touch_ends(jax.random.randint(keys[2], (WINDOWS, POS, READS), 0, QUALS), jax.random.fold_in(keys[2], 1), 0, QUALS - 1).astype(jnp.int32),
        "depth_counts": draw_depth_counts(jax.random.fold_in(keys[10], 71), 0),
        "base_table": normal_values(keys[4], (BASES, C), 0.5, 3.0),
        "qual_table": normal_values(keys[5], (QUALS, C), 0.5, 3.0),
        "value_weight": normal_values(keys[6], (HD, C), C ** -0.5, 0.25),
        "score_weight": draw_score_weight(jax.random.fold_in(keys[10], 71), 0),
        "conv_weight": normal_values(keys[8], (HD, KERNEL, CO), (KERNEL * HD) ** -0.5, 0.078125, ((0, 4),)),
        "cotangent": normal_values(keys[9], (WINDOWS, POS, CO), ((WINDOWS * POS) ** -0.5), 0.15625, ((0, 4), (1, 32))),
    }


def silu_slope(preact):
    sigma = jax.nn.sigmoid(preact)
    return sigma * (1.0 + preact * (1.0 - sigma))


def encode_block(feat_block, base_block, qual_block, depth_block, base_table, qual_table, value_weight, score_weight):
    summed = feat_block.astype(jnp.float32) + jnp.take(base_table.astype(jnp.float32), base_block, axis=0)
    summed = summed + jnp.take(qual_table.astype(jnp.float32), qual_block, axis=0)
    features = lax.optimization_barrier(summed.astype(jnp.bfloat16)).astype(jnp.float32)
    preact = jnp.einsum("prc,jc->prj", features, value_weight.astype(jnp.float32))
    scores = jnp.einsum("prc,ch->prh", features, score_weight.astype(jnp.float32))
    live = (jnp.arange(READS, dtype=jnp.int32)[None, :] < depth_block[:, None])[..., None]
    row_top = jnp.max(jnp.where(live, scores, -1e30), axis=1, keepdims=True)
    expo = jnp.where(live, jnp.exp(scores - row_top), 0.0)
    read_probs = expo / jnp.sum(expo, axis=1, keepdims=True)
    values = lax.optimization_barrier(jax.nn.silu(preact).astype(jnp.bfloat16)).astype(jnp.float32)
    values = values.reshape(P_DEV, READS, HEADS, HEAD_SIZE)
    return features, preact, read_probs, values


def reference(read_feats, base_codes, qual_codes, depth_counts, base_table, qual_table, value_weight, score_weight, conv_weight, cotangent):
    blocks = POS // P_DEV
    half_kernel = KERNEL // 2
    conv_float = conv_weight.astype(jnp.float32)

    def split_rows(array):
        return array.reshape((blocks, P_DEV) + array.shape[1:])

    def one_window(window_args):
        feat_w, base_w, qual_w, depth_w, grad_w = window_args

        def pool_block(block_args):
            features, preact, read_probs, values = encode_block(*block_args, base_table, qual_table, value_weight, score_weight)
            return jnp.einsum("prh,prhe->phe", read_probs, values)

        pooled_exact = lax.map(pool_block, (split_rows(feat_w), split_rows(base_w), split_rows(qual_w), split_rows(depth_w)))
        pooled = lax.optimization_barrier(pooled_exact.reshape(POS, HD).astype(jnp.bfloat16)).astype(jnp.float32)
        grad_float = grad_w.astype(jnp.float32)
        grad_padded = jnp.pad(grad_float, ((half_kernel, half_kernel), (0, 0)))
        pooled_padded = jnp.pad(pooled, ((half_kernel, half_kernel), (0, 0)))
        grad_sum = jnp.zeros((POS, HD), jnp.float32)
        conv_terms = []
        for kernel_tap in range(KERNEL):
            offset = 2 * half_kernel - kernel_tap
            grad_sum = grad_sum + jnp.einsum("qo,io->qi", grad_padded[offset:offset + POS], conv_float[:, kernel_tap, :])
            conv_terms.append(jnp.einsum("pi,po->io", pooled_padded[kernel_tap:kernel_tap + POS], grad_float))
        conv_grad = jnp.stack(conv_terms, axis=1)
        pooled_grad = lax.optimization_barrier(grad_sum.astype(jnp.bfloat16)).astype(jnp.float32)

        def grad_block(carry, block_args):
            feat_b, base_b, qual_b, depth_b, pooled_b, grad_b = block_args
            features, preact, read_probs, values = encode_block(feat_b, base_b, qual_b, depth_b, base_table, qual_table, value_weight, score_weight)
            grad_heads = grad_b.reshape(P_DEV, HEADS, HEAD_SIZE)
            prob_grad = jnp.einsum("prhe,phe->prh", values, grad_heads)
            row_total = jnp.sum(grad_heads * pooled_b, axis=2)
            score_grad = read_probs * (prob_grad - row_total[:, None, :])
            score_grad = lax.optimization_barrier(score_grad.astype(jnp.bfloat16)).astype(jnp.float32)
            value_grad = (read_probs[..., None] * grad_heads[:, None]).reshape(P_DEV, READS, HD) * silu_slope(preact)
            value_grad = lax.optimization_barrier(value_grad.astype(jnp.bfloat16)).astype(jnp.float32)
            value_acc = carry[0] + jnp.einsum("prj,prc->jc", value_grad, features)
            score_acc = carry[1] + jnp.einsum("prc,prh->ch", features, score_grad)
            return (value_acc, score_acc), None

        start_carry = (jnp.zeros((HD, C), jnp.float32), jnp.zeros((C, HEADS), jnp.float32))
        block_inputs = (split_rows(feat_w), split_rows(base_w), split_rows(qual_w), split_rows(depth_w), pooled_exact, split_rows(pooled_grad))
        totals, unused = lax.scan(grad_block, start_carry, block_inputs)
        return totals[0], totals[1], conv_grad

    results = lax.map(one_window, (read_feats, base_codes, qual_codes, depth_counts, cotangent))
    return jnp.sum(results[0], axis=0), jnp.sum(results[1], axis=0), jnp.sum(results[2], axis=0)
```

```python
import jax
import jax.numpy as jnp
from jax import lax
from jax.experimental import pallas as pl
from jax.experimental.pallas import tpu as pltpu
from jax.sharding import Mesh, PartitionSpec as P

AXES = ("depth", "z", "xlo", "xhi", "core")
SEQ = ("z", "xlo")
F32 = jnp.float32
BF16 = jnp.bfloat16
I32 = jnp.int32

TILE = 16
LANES = 128
HEADS = 8
WIDTH = 128
OWN = 2
OWN_UNITS = OWN * WIDTH
UNITS = HEADS * WIDTH
N_DEPTH = 4
N_Z = 16
PLANE = 16


def iota(shape, dim):
    return lax.broadcasted_iota(I32, shape, dim)


def dot(a, b, ca=1, cb=0):
    return lax.dot_general(a, b, (((ca,), (cb,)), ((), ())), preferred_element_type=F32)


def split_pair(value):
    high = value.astype(BF16).astype(F32)
    return high, value - high


def head_spread(lanes, units):
    lane = iota((lanes, units), 0)
    head = iota((lanes, units), 1) // WIDTH
    return ((lane == head) | (lane == head + HEADS)).astype(BF16)


def encode_kernel(
    depth_ref,
    feat_ref,
    codes_ref,
    count_ref,
    table_ref,
    value_ref,
    score_ref,
    features_out,
    values_out,
    slope_out,
    weights_out,
    top_out,
    send_out,
):
    tile, reads, channels = feat_ref.shape
    rows = tile * reads
    code = iota((LANES, rows), 0)
    hot = (code == codes_ref[0, 0:1, :]) | (code == codes_ref[0, 1:2, :] + 8)
    embed = dot(hot.astype(BF16), table_ref[...], 0, 0)
    features = (feat_ref[...].reshape(rows, channels).astype(F32) + embed).astype(BF16)
    features_out[...] = features
    scores = dot(features, score_ref[...]).reshape(tile, reads, LANES)
    read = iota((tile, reads, LANES), 1) + depth_ref[0] * reads
    live = read < count_ref[...][:, None, :]
    top = jnp.max(jnp.where(live, scores, -1e30), axis=1)
    top_high, top_rest = split_pair(top)
    top_low = top_rest.astype(BF16).astype(F32)
    top = top_high + top_low
    weights = jnp.where(live, jnp.exp(scores - top[:, None, :]), 0.0)
    total_high, total_low = split_pair(jnp.sum(weights, axis=1))
    lane = iota((tile, LANES), 1)
    stat = jnp.where(
        lane < 8,
        top_high,
        jnp.where(lane < 16, top_low, jnp.where(lane < 24, total_high, total_low)),
    ).astype(BF16)
    top_out[...] = top
    weights = weights.reshape(rows, LANES)
    weights_out[...] = weights
    high, low = split_pair(weights)
    pair = jnp.where(iota((rows, LANES), 1) < HEADS, high, low).astype(BF16)
    for part in range(N_DEPTH):
        span = slice(part * OWN_UNITS, (part + 1) * OWN_UNITS)
        preact = dot(features, value_ref[span, :], 1, 1)
        lanes = iota((LANES, OWN_UNITS), 0)
        head = iota((LANES, OWN_UNITS), 1) // WIDTH + part * OWN
        spread = ((lanes == head) | (lanes == head + HEADS)).astype(BF16)
        spread = dot(pair, spread)
        sigma = 0.5 * jnp.tanh(0.5 * preact) + 0.5
        values = preact * sigma
        slope = sigma + values * (1.0 - sigma)
        values_out[:, span] = values.astype(BF16)
        slope_out[:, span] = (spread * slope).astype(BF16)
        pool = jnp.sum((spread * values).reshape(tile, reads, OWN_UNITS), axis=1)
        send_out[part, :, 0:OWN_UNITS] = pool.astype(BF16)
        send_out[part, :, OWN_UNITS:] = stat


def encode(depth_index, feats, codes, counts, table, value_weight, score_weight):
    positions, reads, channels = feats.shape
    rows = positions * reads
    step = TILE * reads
    whole = lambda i: (0, 0)
    by_row = lambda i: (i, 0)
    return pl.pallas_call(
        encode_kernel,
        grid=(positions // TILE,),
        in_specs=[
            pl.BlockSpec(memory_space=pltpu.SMEM),
            pl.BlockSpec((TILE, reads, channels), lambda i: (i, 0, 0)),
            pl.BlockSpec((1, 2, step), lambda i: (i, 0, 0)),
            pl.BlockSpec((TILE, LANES), by_row),
            pl.BlockSpec((LANES, channels), whole),
            pl.BlockSpec((UNITS, channels), whole),
            pl.BlockSpec((channels, LANES), whole),
        ],
        out_specs=[
            pl.BlockSpec((step, channels), by_row),
            pl.BlockSpec((step, UNITS), by_row),
            pl.BlockSpec((step, UNITS), by_row),
            pl.BlockSpec((step, LANES), by_row),
            pl.BlockSpec((TILE, LANES), by_row),
            pl.BlockSpec((N_DEPTH, TILE, OWN_UNITS + LANES), lambda i: (0, i, 0)),
        ],
        out_shape=[
            jax.ShapeDtypeStruct((rows, channels), BF16),
            jax.ShapeDtypeStruct((rows, UNITS), BF16),
            jax.ShapeDtypeStruct((rows, UNITS), BF16),
            jax.ShapeDtypeStruct((rows, LANES), F32),
            jax.ShapeDtypeStruct((positions, LANES), F32),
            jax.ShapeDtypeStruct((N_DEPTH, positions, OWN_UNITS + LANES), BF16),
        ],
        compiler_params=pltpu.CompilerParams(vmem_limit_bytes=32 * 2**20),
        cost_estimate=pl.CostEstimate(
            flops=2 * rows * UNITS * (channels + 256),
            bytes_accessed=16 * 2**20,
            transcendentals=rows * UNITS,
        ),
    )(depth_index, feats, codes, counts, table, value_weight, score_weight)


def combine_kernel(depth_ref, recv_ref, grad_ref, payload_out, pooled_out):
    positions = grad_ref.shape[0]
    own = depth_ref[0] * OWN
    lane = iota((LANES, OWN_UNITS), 0)
    head = iota((LANES, OWN_UNITS), 1) // WIDTH + own
    spread_top = ((lane == head) | (lane == head + 8)).astype(BF16)
    spread_total = ((lane == head + 16) | (lane == head + 24)).astype(BF16)
    stats = [recv_ref[d, :, OWN_UNITS:] for d in range(N_DEPTH)]
    tops = [dot(stat, spread_top) for stat in stats]
    top = jnp.maximum(jnp.maximum(tops[0], tops[1]), jnp.maximum(tops[2], tops[3]))
    total = jnp.zeros_like(top)
    pooled = jnp.zeros_like(top)
    for d in range(N_DEPTH):
        scale = jnp.exp(tops[d] - top)
        total += scale * dot(stats[d], spread_total)
        pooled += scale * recv_ref[d, :, 0:OWN_UNITS].astype(F32)
    pooled = pooled / total
    grad = grad_ref[...]
    product = grad.astype(F32) * pooled
    row = iota((OWN_UNITS, OWN_UNITS), 0)
    column = iota((OWN_UNITS, OWN_UNITS), 1)
    source = ((column % 128) // 8) * 16 + (column // 128) * 8 + column % 8
    ordered = dot(pooled.astype(BF16), (row == source).astype(BF16)).astype(BF16)
    pooled_out[0] = ordered[:, 0:128]
    pooled_out[1] = ordered[:, 128:256]
    lane = iota((positions, LANES), 1)
    stat = jnp.zeros((positions, LANES), F32)
    for i in range(OWN):
        span = slice(i * WIDTH, (i + 1) * WIDTH)
        row_total = jnp.sum(product[:, span], axis=1, keepdims=True)
        terms = (top[:, span], total[:, span], jnp.broadcast_to(row_total, (positions, WIDTH)))
        for k, term in enumerate(terms):
            high, low = split_pair(term)
            stat = jnp.where(lane == 4 * k + i, high, stat)
            stat = jnp.where(lane == 4 * k + 2 + i, low, stat)
    stat = stat.astype(BF16)
    for d in range(N_DEPTH):
        payload_out[d, :, 0:OWN_UNITS] = grad
        payload_out[d, :, OWN_UNITS:] = stat


def combine(depth_index, recv, grad):
    positions = grad.shape[0]
    vmem = pl.BlockSpec(memory_space=pltpu.VMEM)
    return pl.pallas_call(
        combine_kernel,
        in_specs=[pl.BlockSpec(memory_space=pltpu.SMEM), vmem, vmem],
        out_specs=[vmem, vmem],
        out_shape=[
            jax.ShapeDtypeStruct(recv.shape, BF16),
            jax.ShapeDtypeStruct((2, positions, 128), BF16),
        ],
        cost_estimate=pl.CostEstimate(flops=10**7, bytes_accessed=500_000, transcendentals=10**5),
    )(depth_index, recv, grad)


def gradient_kernel(
    core_ref,
    payload_ref,
    top_ref,
    weights_ref,
    slope_ref,
    values_ref,
    features_ref,
    mine_out,
    theirs_out,
    total,
    score_total,
):
    step = pl.program_id(0)
    tile = top_ref.shape[0]
    rows, channels = features_ref.shape
    reads = rows // tile
    lane = iota((LANES, LANES), 0)
    target = iota((LANES, LANES), 1)
    joint = [jnp.zeros((tile, LANES), F32) for _ in range(3)]
    for d in range(N_DEPTH):
        stat = payload_ref[d, :, OWN_UNITS:]
        for k in range(3):
            first = (lane // 4 == k) & (target < 2 * HEADS)
            pick = first & (lane % 2 + 2 * d == target % HEADS)
            joint[k] += dot(stat, pick.astype(BF16))
    small = iota((tile, LANES), 1)
    scale = jnp.where(
        small < 2 * HEADS,
        jnp.exp(top_ref[...] - joint[0]) / jnp.where(small < 2 * HEADS, joint[1], 1.0),
        0.0,
    )
    spread = head_spread(LANES, UNITS)
    high, low = split_pair(scale)
    pair = jnp.where(small < HEADS, high, low).astype(BF16)
    scale_units = dot(pair, spread)
    grad = jnp.concatenate(
        [payload_ref[d, :, 0:OWN_UNITS].astype(F32) for d in range(N_DEPTH)], axis=1
    )
    scaled = grad * scale_units
    features = features_ref[...]
    slope = slope_ref[...].astype(F32).reshape(tile, reads, UNITS)
    value_grad = (slope * scaled[:, None, :]).reshape(rows, UNITS).astype(BF16)
    values = values_ref[...].astype(F32).reshape(tile, reads, UNITS)
    product = (values * grad[:, None, :]).reshape(rows, UNITS).astype(BF16)
    prob_grad = dot(product, spread, 1, 1).reshape(tile, reads, LANES)
    weights = weights_ref[...].reshape(tile, reads, LANES)
    score_grad = weights * scale[:, None, :] * (prob_grad - joint[2][:, None, :])
    score_grad = score_grad.reshape(rows, LANES).astype(BF16)

    @pl.when(step == 0)
    def _():
        total[...] = jnp.zeros_like(total)
        score_total[...] = jnp.zeros_like(score_total)

    term = dot(value_grad, features, 0, 0)
    for q in range(4):
        total[q] += term[:, q * 128 : (q + 1) * 128]
    score_total[...] += dot(score_grad, features, 0, 0)

    @pl.when(step == pl.num_programs(0) - 1)
    def _():
        first = core_ref[0] == 0
        for peer in range(PLANE):
            base = (peer // 4) * 256 + (peer % 4) * 4
            for q in range(4):
                for t in range(2):
                    zero = total[q, pl.ds(base + t, N_Z, stride=16), :]
                    one = total[q, pl.ds(base + 2 + t, N_Z, stride=16), :]
                    span = slice(q * 32 + t * 16, q * 32 + t * 16 + 16)
                    mine_out[peer, span, :] = jnp.where(first, zero, one).astype(BF16)
                    theirs_out[peer, span, :] = jnp.where(first, one, zero).astype(BF16)
        score = score_total[0:HEADS, :]
        score = [score[:, q * 128 : (q + 1) * 128] for q in range(4)]
        score = jnp.concatenate(score + [jnp.zeros((96, 128), F32)], axis=0).astype(BF16)
        mine_out[PLANE] = score
        theirs_out[PLANE] = score


def gradients(core_index, payload, top, weights, slope, values, features):
    rows, channels = features.shape
    positions = top.shape[0]
    step = rows // positions * TILE
    by_row = lambda i: (i, 0)
    whole = lambda i: (0, 0, 0)
    shape = (PLANE + 1, 128, 128)
    return pl.pallas_call(
        gradient_kernel,
        grid=(positions // TILE,),
        in_specs=[
            pl.BlockSpec(memory_space=pltpu.SMEM),
            pl.BlockSpec((N_DEPTH, TILE, OWN_UNITS + LANES), lambda i: (0, i, 0)),
            pl.BlockSpec((TILE, LANES), by_row),
            pl.BlockSpec((step, LANES), by_row),
            pl.BlockSpec((step, UNITS), by_row),
            pl.BlockSpec((step, UNITS), by_row),
            pl.BlockSpec((step, channels), by_row),
        ],
        out_specs=[pl.BlockSpec(shape, whole), pl.BlockSpec(shape, whole)],
        out_shape=[jax.ShapeDtypeStruct(shape, BF16)] * 2,
        scratch_shapes=[
            pltpu.VMEM((4, UNITS, 128), F32),
            pltpu.VMEM((LANES, channels), F32),
        ],
        compiler_params=pltpu.CompilerParams(vmem_limit_bytes=32 * 2**20),
        cost_estimate=pl.CostEstimate(
            flops=2 * rows * UNITS * (channels + 256),
            bytes_accessed=16 * 2**20,
            transcendentals=10**4,
        ),
    )(core_index, payload, top, weights, slope, values, features)


def pair_kernel(mine_ref, theirs_ref, send_out):
    score = mine_ref[PLANE, 0:32, :].astype(F32) + theirs_ref[PLANE, 0:32, :].astype(F32)
    score = score.astype(BF16)
    for peer in range(PLANE):
        value = mine_ref[peer].astype(F32) + theirs_ref[peer].astype(F32)
        send_out[peer, 0:128, :] = value.astype(BF16)
        send_out[peer, 128:160, :] = score


def conv_kernel(pooled_ref, grads_ref, part_out):
    peers, positions, _ = pooled_ref.shape
    taps = part_out.shape[1] // 8
    half = taps // 2
    sides = []
    for k in range(taps):
        first = 2 * half - k
        sides.append(
            jnp.concatenate(
                [grads_ref[j].astype(F32)[first : first + positions] for j in range(peers)], axis=0
            ).astype(BF16)
        )
    left = pooled_ref[...].reshape(peers * positions, 128)
    for k in range(taps):
        part = dot(left, sides[k], 0, 0)
        part_out[:, k * 8 : (k + 1) * 8, :] = part.reshape(N_Z, 8, 128)


def line_kernel(recv_ref, conv_ref, send_out, total):
    value = recv_ref[0].astype(F32)
    for peer in range(1, PLANE):
        value += recv_ref[peer].astype(F32)
    total[...] = value
    score = value[128:160]
    for z in range(N_Z):
        block = jnp.concatenate([total[pl.ds(z, 8, stride=16), :], score, conv_ref[z]], axis=0)
        send_out[z] = block.astype(BF16)


def last_kernel(recv_ref, value_out, score_out, conv_out):
    value = recv_ref[0].astype(F32)
    for z in range(1, N_Z):
        value += recv_ref[z].astype(F32)
    for q in range(4):
        span = slice(q * 128, (q + 1) * 128)
        value_out[:, span] = value[2 * q : 2 * q + 2]
        score_out[:, span] = value[8 + 8 * q : 16 + 8 * q]
    for k in range(conv_out.shape[1]):
        conv_out[:, k, :] = value[40 + 8 * k : 48 + 8 * k]


def small_call(kernel, shapes, *operands, scratch=()):
    vmem = pl.BlockSpec(memory_space=pltpu.VMEM)
    single = not isinstance(shapes, list)
    out = pl.pallas_call(
        kernel,
        in_specs=[vmem] * len(operands),
        out_specs=vmem if single else [vmem] * len(shapes),
        out_shape=shapes,
        scratch_shapes=list(scratch),
        cost_estimate=pl.CostEstimate(flops=10**8, bytes_accessed=10**6, transcendentals=0),
    )(*operands)
    return out


def exchange(block, axis):
    return lax.ppermute(block, axis, [(0, 1), (1, 0)])


def body(
    read_feats,
    base_codes,
    qual_codes,
    depth_counts,
    base_table,
    qual_table,
    value_weight,
    score_weight,
    conv_weight,
    cotangent,
):
    _, positions, reads, channels = read_feats.shape
    block_units, taps, outs = conv_weight.shape
    half = taps // 2
    depth_index = lax.axis_index("depth").reshape(1)
    core_index = lax.axis_index("core")
    xhi_index = lax.axis_index("xhi")
    xlo_index = lax.axis_index("xlo")
    rim = positions + 2 * half

    count = lax.axis_size(SEQ)
    forward = [(i, i + 1) for i in range(count - 1)]
    grad_local = cotangent[0]
    low = lax.ppermute(grad_local[-half:], SEQ, forward)
    high = lax.ppermute(grad_local[:half], SEQ, [(b, a) for a, b in forward])
    grad_rim = jnp.concatenate([low, grad_local, high], axis=0)

    empty = LANES - base_table.shape[0] - qual_table.shape[0]
    table = jnp.concatenate([base_table, qual_table, jnp.zeros((empty, channels), BF16)], axis=0)
    score_lanes = jnp.pad(jnp.tile(score_weight, (1, 4)), ((0, 0), (0, LANES - 4 * HEADS)))
    tiles = positions // TILE
    codes = jnp.stack(
        [base_codes[0].reshape(tiles, TILE * reads), qual_codes[0].reshape(tiles, TILE * reads)],
        axis=1,
    )
    counts = jnp.broadcast_to(depth_counts[0][:, None], (positions, LANES))
    features, values, slope, weights, top, pool_send = encode(
        depth_index, read_feats[0], codes, counts, table, value_weight, score_lanes
    )
    pool_recv = lax.all_to_all(pool_send, "depth", split_axis=0, concat_axis=0, tiled=True)

    shifted = [grad_rim[2 * half - k : 2 * half - k + positions] for k in range(taps)]
    block_grad = dot(
        jnp.concatenate(shifted, axis=1), conv_weight.reshape(block_units, taps * outs), 1, 1
    ).astype(BF16)
    payload, pooled = combine(depth_index, pool_recv, block_grad)
    payload = lax.all_to_all(payload, "depth", split_axis=0, concat_axis=0, tiled=True)

    mine, theirs = gradients(
        core_index.reshape(1), payload, top, weights, slope, values, features
    )
    theirs = exchange(theirs, "core")
    plane_send = small_call(
        pair_kernel, jax.ShapeDtypeStruct((PLANE, 160, 128), BF16), mine, theirs
    )
    plane_recv = lax.all_to_all(
        plane_send, ("depth", "xlo", "xhi"), split_axis=0, concat_axis=0, tiled=True
    )

    give = lax.dynamic_index_in_dim(pooled, 1 - xlo_index, 0, keepdims=False)
    keep = lax.dynamic_index_in_dim(pooled, xlo_index, 0, keepdims=False)
    both = jnp.stack([keep, exchange(give, "xlo")])
    both = jnp.concatenate([both, exchange(both, "core")], axis=0)
    pooled = jnp.concatenate([both, exchange(both, "xhi")], axis=0)

    cols = grad_rim.reshape(rim, 2, 2, outs // 4)
    give = lax.dynamic_index_in_dim(cols, 1 - core_index, 2, keepdims=False)
    keep = lax.dynamic_index_in_dim(cols, core_index, 2, keepdims=False)
    both = jnp.stack([keep, exchange(give, "core")])
    give = lax.dynamic_index_in_dim(both, 1 - xhi_index, 2, keepdims=False)
    keep = lax.dynamic_index_in_dim(both, xhi_index, 2, keepdims=False)
    both = jnp.stack([keep, exchange(give, "xhi")])
    both = both.reshape(4, rim, outs // 4)
    grads = jnp.stack([both, exchange(both, "xlo")], axis=1).reshape(8, rim, outs // 4)

    conv_part = small_call(
        conv_kernel, jax.ShapeDtypeStruct((N_Z, 8 * taps, 128), F32), pooled, grads
    )

    line_send = small_call(
        line_kernel,
        jax.ShapeDtypeStruct((N_Z, 40 + 8 * taps, 128), BF16),
        plane_recv,
        conv_part,
        scratch=[pltpu.VMEM((160, 128), F32)],
    )
    line_recv = lax.all_to_all(line_send, "z", split_axis=0, concat_axis=0, tiled=True)
    value_weight_grad, score_weight_grad, conv_weight_grad = small_call(
        last_kernel,
        [
            jax.ShapeDtypeStruct((2, channels), F32),
            jax.ShapeDtypeStruct((HEADS, channels), F32),
            jax.ShapeDtypeStruct((8, taps, 128), F32),
        ],
        line_recv,
    )
    return (value_weight_grad, score_weight_grad.T, conv_weight_grad)


def solution(mesh):
    fine = Mesh(mesh.devices.reshape(N_DEPTH, N_Z, 2, 2, 2), AXES)
    rep = ("xhi", "core")
    placed = (
        P(rep, SEQ, "depth", None),
        P(rep, SEQ, "depth"),
        P(rep, SEQ, "depth"),
        P(rep, SEQ),
        P(),
        P(),
        P(),
        P(),
        P("depth", None, None),
        P(rep, SEQ, None),
    )
    return jax.shard_map(
        body,
        mesh=fine,
        in_specs=placed,
        out_specs=(P(AXES, None), P(), P(("depth",) + SEQ, None, rep)),
        check_vma=False,
    )
```

```python
import jax
import jax.numpy as jnp
from jax import lax
from jax.experimental import pallas as pl
from jax.experimental.pallas import tpu as pltpu
from jax.sharding import Mesh, PartitionSpec as P

AXES = ("depth", "z", "xlo", "xhi", "core")
SEQ = ("z", "xlo")
F32 = jnp.float32
BF16 = jnp.bfloat16
I32 = jnp.int32

TILE = 16
LANES = 128
HEADS = 8
WIDTH = 128
OWN = 2
OWN_UNITS = OWN * WIDTH
UNITS = HEADS * WIDTH
RIM = 80
N_DEPTH = 4
N_Z = 16
PLANE = 16


def iota(shape, dim):
    return lax.broadcasted_iota(I32, shape, dim)


def dot(a, b, ca=1, cb=0):
    return lax.dot_general(a, b, (((ca,), (cb,)), ((), ())), preferred_element_type=F32)


def split_pair(value):
    high = value.astype(BF16).astype(F32)
    return high, value - high


def encode_kernel(
    depth_ref,
    feat_hbm,
    value_hbm,
    base_codes_ref,
    qual_codes_ref,
    count_ref,
    base_ref,
    qual_ref,
    score_ref,
    bulk_out,
    weights_out,
    top_out,
    send_out,
    feat_buf,
    value_buf,
    bulk,
    in_sems,
    out_sems,
):
    positions, reads, channels = feat_buf.shape
    tiles = positions // TILE
    rows = TILE * reads
    copies, stores = [], []
    for i in range(tiles):
        span = pl.ds(i * TILE, TILE)
        copies.append(pltpu.make_async_copy(feat_hbm.at[span], feat_buf.at[span], in_sems.at[i]))
        span = pl.ds(i * rows, rows)
        stores.append(pltpu.make_async_copy(bulk.at[span], bulk_out.at[span], out_sems.at[i]))
    copies.append(pltpu.make_async_copy(value_hbm, value_buf, in_sems.at[tiles]))
    for i in (0, tiles) + tuple(range(1, tiles)):
        copies[i].start()
    n_qual, n_base = qual_ref.shape[0], base_ref.shape[0]
    place = (iota((LANES, n_qual), 0) == iota((LANES, n_qual), 1)).astype(BF16)
    table = dot(place, qual_ref[...])
    place = (iota((LANES, n_base), 0) == iota((LANES, n_base), 1) + 96).astype(BF16)
    table = (table + dot(place, base_ref[...])).astype(BF16)
    slot = iota((LANES, HEADS), 0)
    place = (slot % HEADS == iota((LANES, HEADS), 1)) & (slot < 4 * HEADS)
    score_weight = dot(place.astype(BF16), score_ref[...]).astype(BF16)
    ones = jnp.ones((positions, LANES), BF16)
    spreads = []
    for part in range(N_DEPTH):
        lanes = iota((LANES, OWN_UNITS), 0)
        head = iota((LANES, OWN_UNITS), 1) // WIDTH + part * OWN
        spreads.append(((lanes == head) | (lanes == head + HEADS)).astype(BF16))
    base_codes = base_codes_ref[...].astype(F32)
    qual_codes = qual_codes_ref[...].astype(F32)
    counts = count_ref[...].astype(F32)
    lane = iota((rows, LANES), 1).astype(F32)
    for i in range(tiles):
        span = slice(i * TILE, (i + 1) * TILE)
        row_span = slice(i * rows, (i + 1) * rows)
        shape = (TILE, reads, positions)
        at = iota(shape, 2) == iota(shape, 0) + i * TILE
        base = jnp.where(at, base_codes[None], 0.0).reshape(rows, positions).astype(BF16)
        qual = jnp.where(at, qual_codes[None], 0.0).reshape(rows, positions).astype(BF16)
        shape = (TILE, positions)
        at = iota(shape, 1) == iota(shape, 0) + i * TILE
        count = dot(jnp.where(at, counts, 0.0).astype(BF16), ones)
        hot = (dot(qual, ones) == lane) | (dot(base, ones) + 96.0 == lane)
        embed = dot(hot.astype(BF16), table)
        copies[i].wait()
        features = feat_buf[span].reshape(rows, channels).astype(F32) + embed
        features = features.astype(BF16)
        bulk[row_span, 2 * UNITS :] = features
        scores = dot(features, score_weight, 1, 1).reshape(TILE, reads, LANES)
        read = iota((TILE, reads, LANES), 1) + depth_ref[0] * reads
        live = read < count.astype(I32)[:, None, :]
        top = jnp.max(jnp.where(live, scores, -1e30), axis=1)
        top_high, top_rest = split_pair(top)
        top_low = top_rest.astype(BF16).astype(F32)
        top = top_high + top_low
        weights = jnp.where(live, jnp.exp(scores - top[:, None, :]), 0.0)
        total_high, total_low = split_pair(jnp.sum(weights, axis=1))
        small = iota((TILE, LANES), 1)
        stat = jnp.where(
            small < 8,
            top_high,
            jnp.where(small < 16, top_low, jnp.where(small < 24, total_high, total_low)),
        ).astype(BF16)
        top_out[span, :] = top
        weights = weights.reshape(rows, LANES)
        weights_out[row_span, :] = weights
        high, low = split_pair(weights)
        pair = jnp.where(iota((rows, LANES), 1) < HEADS, high, low).astype(BF16)
        if i == 0:
            copies[tiles].wait()
        for part in range(N_DEPTH):
            cols = slice(part * OWN_UNITS, (part + 1) * OWN_UNITS)
            preact = dot(features, value_buf[cols, :], 1, 1).astype(BF16)
            spread = dot(pair, spreads[part]).astype(BF16)
            sigma = 0.5 * jnp.tanh(0.5 * preact) + 0.5
            values = preact * sigma
            slope = sigma + values * (1.0 - sigma)
            bulk[row_span, cols] = spread * slope
            bulk[row_span, UNITS + part * OWN_UNITS : UNITS + (part + 1) * OWN_UNITS] = values
            pool = (spread * values).astype(F32).reshape(TILE, reads, OWN_UNITS)
            send_out[part, span, 0:OWN_UNITS] = jnp.sum(pool, axis=1).astype(BF16)
            send_out[part, span, OWN_UNITS:] = stat
        stores[i].start()
    for store in stores:
        store.wait()


VMEM = pl.BlockSpec(memory_space=pltpu.VMEM)
SMEM = pl.BlockSpec(memory_space=pltpu.SMEM)
HBM = pl.BlockSpec(memory_space=pltpu.HBM)
ANY = pl.BlockSpec(memory_space=pl.ANY)


def in_hbm(*arrays):
    return [pltpu.with_memory_space_constraint(array, pltpu.HBM) for array in arrays]


def encode(depth_index, feats, value_weight, *rest):
    positions, reads, channels = feats.shape
    rows = positions * reads
    width = 2 * UNITS + channels
    return pl.pallas_call(
        encode_kernel,
        in_specs=[SMEM, HBM, HBM] + [VMEM] * 6,
        out_specs=[HBM] + [VMEM] * 3,
        out_shape=[
            pltpu.HBM((rows, width), BF16),
            jax.ShapeDtypeStruct((rows, LANES), F32),
            jax.ShapeDtypeStruct((positions, LANES), F32),
            jax.ShapeDtypeStruct((N_DEPTH, positions, OWN_UNITS + LANES), BF16),
        ],
        scratch_shapes=[
            pltpu.VMEM(feats.shape, BF16),
            pltpu.VMEM(value_weight.shape, BF16),
            pltpu.VMEM((rows, width), BF16),
            pltpu.SemaphoreType.DMA((positions // TILE + 1,)),
            pltpu.SemaphoreType.DMA((positions // TILE,)),
        ],
        compiler_params=pltpu.CompilerParams(vmem_limit_bytes=36 * 2**20),
        cost_estimate=pl.CostEstimate(
            flops=2 * rows * UNITS * (channels + 256),
            bytes_accessed=16 * 2**20,
            transcendentals=rows * UNITS,
        ),
    )(depth_index, *in_hbm(feats, value_weight, *rest))


def rim_kernel(low_ref, local_ref, high_ref, weight_ref, grad_out, cols_out):
    positions, outs = local_ref.shape
    taps = weight_ref.shape[0]
    half = taps // 2
    rows = cols_out.shape[1]
    rim = jnp.concatenate(
        [
            low_ref[...].astype(F32),
            local_ref[...].astype(F32),
            high_ref[...].astype(F32),
            jnp.zeros((rows - positions - 2 * half, outs), F32),
        ],
        axis=0,
    ).astype(BF16)
    grad = jnp.zeros((positions, OWN_UNITS), F32)
    for k in range(taps):
        first = 2 * half - k
        grad += dot(rim, weight_ref[k], 1, 1)[first : first + positions]
    grad_out[...] = grad.astype(BF16)
    for i in range(cols_out.shape[0]):
        cols_out[i] = rim[:, i * 128 : (i + 1) * 128]


def combine_kernel(depth_ref, recv_ref, grad_ref, cols_ref, payload_out, gather_out):
    positions = grad_ref.shape[0]
    own = depth_ref[0] * OWN
    lane = iota((LANES, OWN_UNITS), 0)
    head = iota((LANES, OWN_UNITS), 1) // WIDTH + own
    spread_top = ((lane == head) | (lane == head + 8)).astype(BF16)
    spread_total = ((lane == head + 16) | (lane == head + 24)).astype(BF16)
    stats = [recv_ref[d, :, OWN_UNITS:] for d in range(N_DEPTH)]
    tops = [dot(stat, spread_top) for stat in stats]
    top = jnp.maximum(jnp.maximum(tops[0], tops[1]), jnp.maximum(tops[2], tops[3]))
    total = jnp.zeros_like(top)
    pooled = jnp.zeros_like(top)
    for d in range(N_DEPTH):
        scale = jnp.exp(tops[d] - top)
        total += scale * dot(stats[d], spread_total)
        pooled += scale * recv_ref[d, :, 0:OWN_UNITS].astype(F32)
    pooled = pooled / total
    grad = grad_ref[...]
    product = grad.astype(F32) * pooled
    row = iota((OWN_UNITS, OWN_UNITS), 0)
    column = iota((OWN_UNITS, OWN_UNITS), 1)
    source = ((column % 128) // 8) * 16 + (column // 128) * 8 + column % 8
    ordered = dot(pooled.astype(BF16), (row == source).astype(BF16))
    ordered = ordered.astype(BF16)
    for peer in range(8):
        xlo = peer // 4
        gather_out[peer, 0:positions, :] = ordered[:, xlo * 128 : (xlo + 1) * 128]
        gather_out[peer, positions:, :] = cols_ref[peer % 4]
    lane = iota((positions, LANES), 1)
    stat = jnp.zeros((positions, LANES), F32)
    for i in range(OWN):
        span = slice(i * WIDTH, (i + 1) * WIDTH)
        row_total = jnp.sum(product[:, span], axis=1, keepdims=True)
        terms = (top[:, span], total[:, span], jnp.broadcast_to(row_total, (positions, WIDTH)))
        for k, term in enumerate(terms):
            high, low = split_pair(term)
            stat = jnp.where(lane == 4 * k + i, high, stat)
            stat = jnp.where(lane == 4 * k + 2 + i, low, stat)
    stat = stat.astype(BF16)
    for d in range(N_DEPTH):
        payload_out[d, :, 0:OWN_UNITS] = grad
        payload_out[d, :, OWN_UNITS:] = stat


def gradient_kernel(
    core_ref,
    payload_ref,
    top_ref,
    weights_ref,
    bulk_hbm,
    mine_out,
    theirs_out,
    total,
    slope_buf,
    values_buf,
    features_buf,
    sems,
):
    positions = top_ref.shape[0]
    rows, channels = features_buf.shape
    reads = rows // positions
    copies = [
        pltpu.make_async_copy(bulk_hbm.at[:, pl.ds(2 * UNITS, channels)], features_buf, sems.at[0])
    ]
    for d in range(N_DEPTH):
        for k, buf in enumerate((slope_buf, values_buf)):
            cols = pl.ds(k * UNITS + d * OWN_UNITS, OWN_UNITS)
            copies.append(
                pltpu.make_async_copy(bulk_hbm.at[:, cols], buf.at[d], sems.at[1 + 2 * d + k])
            )
    for i in [1, 0] + list(range(2, len(copies))):
        copies[i].start()
    lane = iota((LANES, LANES), 0)
    target = iota((LANES, LANES), 1)
    joint = [jnp.zeros((positions, LANES), F32) for _ in range(3)]
    for d in range(N_DEPTH):
        stat = payload_ref[d, :, OWN_UNITS:]
        for k in range(3):
            first = (lane // 4 == k) & (target < 2 * HEADS)
            pick = first & (lane % 2 + 2 * d == target % HEADS)
            joint[k] += dot(stat, pick.astype(BF16))
    small = iota((positions, LANES), 1)
    scale = jnp.where(
        small < 2 * HEADS,
        jnp.exp(top_ref[...] - joint[0]) / jnp.where(small < 2 * HEADS, joint[1], 1.0),
        0.0,
    )
    high, low = split_pair(scale)
    pair = jnp.where(small < HEADS, high, low).astype(BF16)
    first = core_ref[0] == 0

    def by_read(block):
        shape = (positions, 16, OWN_UNITS)
        return jnp.broadcast_to(block[:, None, :], shape).astype(BF16)[:, None]

    split = (positions, reads // 16, 16, OWN_UNITS)
    prob_grad = jnp.zeros((rows, LANES), F32)
    for d in range(N_DEPTH):
        cols = slice(d * OWN_UNITS, (d + 1) * OWN_UNITS)
        lanes = iota((LANES, OWN_UNITS), 0)
        head = iota((LANES, OWN_UNITS), 1) // WIDTH + d * OWN
        spread = ((lanes == head) | (lanes == head + HEADS)).astype(BF16)
        grad = payload_ref[d, :, 0:OWN_UNITS].astype(F32)
        scaled = by_read(grad * dot(pair, spread))
        copies[1 + 2 * d].wait()
        value_grad = (slope_buf[d].reshape(split) * scaled).reshape(rows, OWN_UNITS)
        if d == 0:
            copies[0].wait()
        term = dot(value_grad, features_buf[...], 0, 0)
        for q in range(4):
            total[q, cols, :] = term[:, q * 128 : (q + 1) * 128]
        copies[2 + 2 * d].wait()
        product = (values_buf[d].reshape(split) * by_read(grad)).reshape(rows, OWN_UNITS)
        prob_grad += dot(product, spread, 1, 1)
        for peer in range(4 * d, 4 * d + 4):
            base = d * OWN_UNITS + (peer % 4) * 4
            for q in range(4):
                for t in range(2):
                    zero = total[q, pl.ds(base + t, N_Z, stride=16), :]
                    one = total[q, pl.ds(base + 2 + t, N_Z, stride=16), :]
                    span = slice(q * 32 + t * 16, q * 32 + t * 16 + 16)
                    mine_out[peer, span, :] = jnp.where(first, zero, one).astype(BF16)
                    theirs_out[peer, span, :] = jnp.where(first, one, zero).astype(BF16)
    weights = weights_ref[...].reshape(positions, reads, LANES)
    prob_grad = prob_grad.reshape(positions, reads, LANES)
    score_grad = weights * scale[:, None, :] * (prob_grad - joint[2][:, None, :])
    score_grad = score_grad.reshape(rows, LANES).astype(BF16)
    score = dot(score_grad, features_buf[...], 0, 0)[0:HEADS]
    score = [score[:, q * 128 : (q + 1) * 128] for q in range(4)]
    score = jnp.concatenate(score + [jnp.zeros((96, 128), F32)], axis=0).astype(BF16)
    mine_out[PLANE] = score
    theirs_out[PLANE] = score


def gradients(core_index, payload, top, weights, bulk, channels):
    rows = bulk.shape[0]
    shape = (PLANE + 1, 128, 128)
    return pl.pallas_call(
        gradient_kernel,
        in_specs=[SMEM] + [VMEM] * 3 + [HBM],
        out_specs=[VMEM, VMEM],
        out_shape=[jax.ShapeDtypeStruct(shape, BF16)] * 2,
        scratch_shapes=[
            pltpu.VMEM((4, UNITS, 128), F32),
            pltpu.VMEM((N_DEPTH, rows, OWN_UNITS), BF16),
            pltpu.VMEM((N_DEPTH, rows, OWN_UNITS), BF16),
            pltpu.VMEM((rows, channels), BF16),
            pltpu.SemaphoreType.DMA((1 + 2 * N_DEPTH,)),
        ],
        compiler_params=pltpu.CompilerParams(vmem_limit_bytes=36 * 2**20),
        cost_estimate=pl.CostEstimate(
            flops=2 * rows * UNITS * (channels + 256),
            bytes_accessed=16 * 2**20,
            transcendentals=10**4,
        ),
    )(core_index, payload, top, weights, *in_hbm(bulk))


def pair_kernel(mine_ref, theirs_ref, send_out):
    score = mine_ref[PLANE, 0:32, :].astype(F32) + theirs_ref[PLANE, 0:32, :].astype(F32)
    score = score.astype(BF16)
    for peer in range(PLANE):
        value = mine_ref[peer].astype(F32) + theirs_ref[peer].astype(F32)
        send_out[peer, 0:128, :] = value.astype(BF16)
        send_out[peer, 128:160, :] = score


def conv_kernel(recv_ref, part_out):
    peers = recv_ref.shape[0]
    positions = recv_ref.shape[1] - RIM
    taps = part_out.shape[1] // 8
    half = taps // 2
    left = recv_ref[:, 0:positions, :].reshape(peers * positions, 128)
    grads = [recv_ref[j, positions:, :].astype(F32) for j in range(peers)]
    for k in range(taps):
        first = 2 * half - k
        shifted = jnp.concatenate([grad[first : first + positions] for grad in grads], axis=0)
        part = dot(left, shifted.astype(BF16), 0, 0)
        part_out[:, k * 8 : (k + 1) * 8, :] = part.reshape(N_Z, 8, 128)


def line_kernel(recv_ref, conv_ref, send_out, total):
    value = recv_ref[0].astype(F32)
    for peer in range(1, PLANE):
        value += recv_ref[peer].astype(F32)
    total[...] = value
    score = value[128:160]
    for z in range(N_Z):
        block = jnp.concatenate([total[pl.ds(z, 8, stride=16), :], score, conv_ref[z]], axis=0)
        send_out[z] = block.astype(BF16)


def last_kernel(recv_ref, value_out, score_out, conv_out):
    value = recv_ref[0].astype(F32)
    for z in range(1, N_Z):
        value += recv_ref[z].astype(F32)
    for q in range(4):
        span = slice(q * 128, (q + 1) * 128)
        value_out[:, span] = value[2 * q : 2 * q + 2]
        score_out[:, span] = value[8 + 8 * q : 16 + 8 * q]
    for k in range(conv_out.shape[0]):
        conv_out[k] = value[40 + 8 * k : 48 + 8 * k]


def small_call(kernel, shapes, *operands, specs=None, scratch=(), mib=6):
    single = not isinstance(shapes, list)
    return pl.pallas_call(
        kernel,
        in_specs=specs or [VMEM] * len(operands),
        out_specs=VMEM if single else [VMEM] * len(shapes),
        out_shape=shapes,
        scratch_shapes=list(scratch),
        compiler_params=pltpu.CompilerParams(vmem_limit_bytes=mib * 2**20),
        cost_estimate=pl.CostEstimate(flops=10**8, bytes_accessed=10**6, transcendentals=0),
    )(*operands)


def exchange(block, axis):
    return lax.ppermute(block, axis, [(0, 1), (1, 0)])


def body(
    read_feats,
    base_codes,
    qual_codes,
    depth_counts,
    base_table,
    qual_table,
    value_weight,
    score_weight,
    conv_weight,
    cotangent,
):
    _, positions, reads, channels = read_feats.shape
    block_units, taps, outs = conv_weight.shape
    half = taps // 2
    depth_index = lax.axis_index("depth")
    core_index = lax.axis_index("core")
    def shaped(*shape, kind=BF16):
        return jax.ShapeDtypeStruct(shape, kind)

    count = lax.axis_size(SEQ)
    forward = [(i, i + 1) for i in range(count - 1)]
    grad_local = cotangent[0]
    low = lax.ppermute(grad_local[-half:], SEQ, forward)
    high = lax.ppermute(grad_local[:half], SEQ, [(b, a) for a, b in forward])

    bulk, weights, top, pool_send = encode(
        depth_index.reshape(1),
        read_feats[0],
        value_weight,
        base_codes[0].T,
        qual_codes[0].T,
        depth_counts,
        base_table,
        qual_table,
        score_weight.T,
    )
    pool_recv = lax.all_to_all(pool_send, "depth", split_axis=0, concat_axis=0, tiled=True)

    block_grad, cols = small_call(
        rim_kernel,
        [shaped(positions, block_units), shaped(4, RIM, 128)],
        low,
        grad_local,
        high,
        conv_weight.transpose(1, 0, 2),
    )
    payload, gather_send = small_call(
        combine_kernel,
        [shaped(*pool_send.shape), shaped(8, positions + RIM, 128)],
        depth_index.reshape(1),
        pool_recv,
        block_grad,
        cols,
        specs=[SMEM] + [VMEM] * 3,
    )
    payload = lax.all_to_all(payload, "depth", split_axis=0, concat_axis=0, tiled=True)

    payload, gather_send = lax.optimization_barrier((payload, gather_send))
    gather_recv = lax.all_to_all(
        gather_send, ("xlo", "xhi", "core"), split_axis=0, concat_axis=0, tiled=True
    )

    mine, theirs = gradients(core_index.reshape(1), payload, top, weights, bulk, channels)
    theirs = exchange(theirs, "core")
    plane_send = small_call(pair_kernel, shaped(PLANE, 160, 128), mine, theirs)
    plane_recv = lax.all_to_all(
        plane_send, ("depth", "xlo", "xhi"), split_axis=0, concat_axis=0, tiled=True
    )
    conv_part = small_call(conv_kernel, shaped(N_Z, 8 * taps, 128, kind=F32), gather_recv)

    line_send = small_call(
        line_kernel,
        shaped(N_Z, 40 + 8 * taps, 128),
        plane_recv,
        conv_part,
        scratch=[pltpu.VMEM((160, 128), F32)],
    )
    line_recv = lax.all_to_all(line_send, "z", split_axis=0, concat_axis=0, tiled=True)
    value_weight_grad, score_weight_grad, conv_weight_grad = small_call(
        last_kernel,
        [
            shaped(2, channels, kind=F32),
            shaped(HEADS, channels, kind=F32),
            shaped(taps, 8, 128, kind=F32),
        ],
        line_recv,
    )
    return (value_weight_grad, score_weight_grad.T, conv_weight_grad.transpose(1, 0, 2))


def solution(mesh):
    fine = Mesh(mesh.devices.reshape(N_DEPTH, N_Z, 2, 2, 2), AXES)
    rep = ("xhi", "core")
    placed = (
        P(rep, SEQ, "depth", None),
        P(rep, SEQ, "depth"),
        P(rep, SEQ, "depth"),
        P(rep, SEQ),
        P(),
        P(),
        P(),
        P(),
        P("depth", None, None),
        P(rep, SEQ, None),
    )
    return jax.shard_map(
        body,
        mesh=fine,
        in_specs=placed,
        out_specs=(P(AXES, None), P(), P(("depth",) + SEQ, None, rep)),
        check_vma=False,
    )
```

```python
import jax
import jax.numpy as jnp
from jax import lax
from jax.experimental import pallas as pl
from jax.experimental.pallas import tpu as pltpu
from jax.sharding import Mesh, PartitionSpec as P

AXES = ("depth", "z", "xlo", "xhi", "core")
SEQ = ("z", "xlo")
F32 = jnp.float32
BF16 = jnp.bfloat16
I32 = jnp.int32

TILE = 16
LANES = 128
HEADS = 8
WIDTH = 128
OWN = 2
OWN_UNITS = OWN * WIDTH
UNITS = HEADS * WIDTH
RIM = 80
N_DEPTH = 4
N_Z = 16
PLANE = 16


def iota(shape, dim):
    return lax.broadcasted_iota(I32, shape, dim)


def dot(a, b, ca=1, cb=0):
    return lax.dot_general(a, b, (((ca,), (cb,)), ((), ())), preferred_element_type=F32)


def split_pair(value):
    high = value.astype(BF16).astype(F32)
    return high, value - high


def encode_kernel(
    depth_ref,
    count_ref,
    feat_hbm,
    value_hbm,
    base_codes_ref,
    qual_codes_ref,
    base_ref,
    qual_ref,
    score_ref,
    features_out,
    slope_out,
    values_out,
    pair_out,
    top_out,
    stat_out,
    pool_out,
    feat_buf,
    value_buf,
    features_buf,
    slope_buf,
    values_buf,
    hot_buf,
    embed_buf,
    score_buf,
    stat_buf,
    pair_buf,
    preact_buf,
    spread_buf,
    in_sems,
    out_sems,
):
    positions, reads, channels = feat_buf.shape
    tiles = positions // TILE
    rows = TILE * reads
    copies = []
    for i in range(tiles):
        span = pl.ds(i * TILE, TILE)
        copies.append(pltpu.make_async_copy(feat_hbm.at[span], feat_buf.at[span], in_sems.at[i]))
    copies.append(pltpu.make_async_copy(value_hbm, value_buf, in_sems.at[tiles]))
    for i in (0, tiles) + tuple(range(1, tiles)):
        copies[i].start()
    n_qual, n_base = qual_ref.shape[0], base_ref.shape[0]
    place = (iota((LANES, n_qual), 0) == iota((LANES, n_qual), 1)).astype(BF16)
    table = dot(place, qual_ref[...])
    place = (iota((LANES, n_base), 0) == iota((LANES, n_base), 1) + 96).astype(BF16)
    table = (table + dot(place, base_ref[...])).astype(BF16)
    slot = iota((LANES, HEADS), 0)
    place = (slot % HEADS == iota((LANES, HEADS), 1)) & (slot < 4 * HEADS)
    score_weight = dot(place.astype(BF16), score_ref[...]).astype(BF16)
    spreads = []
    for part in range(N_DEPTH):
        lanes = iota((LANES, OWN_UNITS), 0)
        head = iota((LANES, OWN_UNITS), 1) // WIDTH + part * OWN
        spreads.append(((lanes == head) | (lanes == head + HEADS)).astype(BF16))
    lane = iota((reads, LANES), 1)
    read = iota((reads, LANES), 0) + depth_ref[0] * reads
    for i in range(tiles):
        first_row = i * rows
        for p in range(TILE):
            at = i * TILE + p
            qual = jnp.broadcast_to(qual_codes_ref[:, at : at + 1], (reads, LANES))
            base = jnp.broadcast_to(base_codes_ref[:, at : at + 1], (reads, LANES))
            hot = (lane == qual) | (lane == base + 96)
            hot_buf[p * reads : (p + 1) * reads, :] = hot.astype(BF16)
        embed_buf[...] = dot(hot_buf[...], table)
        copies[i].wait()
        for p in range(TILE):
            near = slice(p * reads, (p + 1) * reads)
            feature = feat_buf[i * TILE + p].astype(F32) + embed_buf[near, :]
            far = slice(first_row + p * reads, first_row + (p + 1) * reads)
            features_buf[far, :] = feature.astype(BF16)
    stores = [pltpu.make_async_copy(features_buf, features_out, out_sems.at[0])]
    stores[0].start()
    features = features_buf[...]
    score_buf[...] = dot(features, score_weight, 1, 1)
    for p in range(positions):
        near = slice(p * reads, (p + 1) * reads)
        scores = score_buf[near, :]
        live = read < count_ref[p]
        top = jnp.max(jnp.where(live, scores, -1e30), axis=0, keepdims=True)
        top_high, top_rest = split_pair(top)
        top_low = top_rest.astype(BF16).astype(F32)
        top = top_high + top_low
        weights = jnp.where(live, jnp.exp(scores - top), 0.0)
        total_high, total_low = split_pair(jnp.sum(weights, axis=0, keepdims=True))
        small = lane[0:1]
        stat_buf[p : p + 1, :] = jnp.where(
            small < 8,
            top_high,
            jnp.where(small < 16, top_low, jnp.where(small < 24, total_high, total_low)),
        )
        top_out[p : p + 1, :] = top
        high, low = split_pair(weights)
        pair_buf[near, :] = jnp.where(lane < HEADS, high, low).astype(BF16)
    stores.append(pltpu.make_async_copy(pair_buf, pair_out, out_sems.at[1 + 2 * N_DEPTH]))
    stores[1].start()
    copies[tiles].wait()
    stat_out[...] = stat_buf[...].astype(BF16)

    def multiply(part):
        cols = slice(part * OWN_UNITS, (part + 1) * OWN_UNITS)
        preact_buf[part % 2] = dot(features, value_buf[cols, :], 1, 1)
        spread_buf[part % 2] = dot(pair_buf[...], spreads[part])

    multiply(0)
    for part in range(N_DEPTH):
        if part + 1 < N_DEPTH:
            multiply(part + 1)
        cols = slice(part * OWN_UNITS, (part + 1) * OWN_UNITS)
        for p in range(positions):
            near = slice(p * reads, (p + 1) * reads)
            preact = preact_buf[part % 2, near, :].astype(BF16)
            spread = spread_buf[part % 2, near, :].astype(BF16)
            sigma = 0.5 * jnp.tanh(0.5 * preact) + 0.5
            values = preact * sigma
            slope = sigma + values * (1.0 - sigma)
            slope_buf[part, near, :] = spread * slope
            values_buf[part, near, :] = values
            pool = jnp.sum((spread * values).astype(F32), axis=0, keepdims=True)
            pool_out[p : p + 1, cols] = pool
        for k, (buf, out) in enumerate(((slope_buf, slope_out), (values_buf, values_out))):
            store = pltpu.make_async_copy(buf.at[part], out.at[part], out_sems.at[1 + 2 * part + k])
            store.start()
            stores.append(store)
    for store in stores:
        store.wait()


VMEM = pl.BlockSpec(memory_space=pltpu.VMEM)
SMEM = pl.BlockSpec(memory_space=pltpu.SMEM)
HBM = pl.BlockSpec(memory_space=pltpu.HBM)
ANY = pl.BlockSpec(memory_space=pl.ANY)


def in_hbm(*arrays):
    return [pltpu.with_memory_space_constraint(array, pltpu.HBM) for array in arrays]


def encode(depth_index, counts, feats, value_weight, *rest):
    positions, reads, channels = feats.shape
    rows = positions * reads
    step = TILE * reads
    return pl.pallas_call(
        encode_kernel,
        in_specs=[SMEM, SMEM, HBM, HBM] + [VMEM] * 5,
        out_specs=[HBM] * 4 + [VMEM] * 3,
        out_shape=[
            pltpu.HBM((rows, channels), BF16),
            pltpu.HBM((N_DEPTH, rows, OWN_UNITS), BF16),
            pltpu.HBM((N_DEPTH, rows, OWN_UNITS), BF16),
            pltpu.HBM((rows, LANES), BF16),
            jax.ShapeDtypeStruct((positions, LANES), F32),
            jax.ShapeDtypeStruct((positions, LANES), BF16),
            jax.ShapeDtypeStruct((positions, UNITS), F32),
        ],
        scratch_shapes=[
            pltpu.VMEM(feats.shape, BF16),
            pltpu.VMEM(value_weight.shape, BF16),
            pltpu.VMEM((rows, channels), BF16),
            pltpu.VMEM((N_DEPTH, rows, OWN_UNITS), BF16),
            pltpu.VMEM((N_DEPTH, rows, OWN_UNITS), BF16),
            pltpu.VMEM((step, LANES), BF16),
            pltpu.VMEM((step, channels), F32),
            pltpu.VMEM((rows, LANES), F32),
            pltpu.VMEM((positions, LANES), F32),
            pltpu.VMEM((rows, LANES), BF16),
            pltpu.VMEM((2, rows, OWN_UNITS), F32),
            pltpu.VMEM((2, rows, OWN_UNITS), F32),
            pltpu.SemaphoreType.DMA((positions // TILE + 1,)),
            pltpu.SemaphoreType.DMA((2 + 2 * N_DEPTH,)),
        ],
        compiler_params=pltpu.CompilerParams(vmem_limit_bytes=36 * 2**20),
        cost_estimate=pl.CostEstimate(
            flops=2 * rows * UNITS * (channels + 256),
            bytes_accessed=16 * 2**20,
            transcendentals=rows * UNITS,
        ),
    )(depth_index, *in_hbm(counts, feats, value_weight, *rest))


def rim_kernel(low_ref, local_ref, high_ref, weight_ref, stat_ref, payload_out, cols_out):
    positions, outs = local_ref.shape
    taps = weight_ref.shape[0]
    half = taps // 2
    rows = cols_out.shape[1]
    low, high = low_ref[...].astype(F32), high_ref[...].astype(F32)
    local = local_ref[...].astype(F32)
    pad = jnp.zeros((rows - positions - 2 * half, outs), F32)
    rim = jnp.concatenate([low, local, high, pad], axis=0).astype(BF16)
    cols = jnp.concatenate([local, low, high, pad], axis=0).astype(BF16)
    grad = jnp.zeros((positions, OWN_UNITS), F32)
    for k in range(taps):
        first = 2 * half - k
        grad += dot(rim, weight_ref[k], 1, 1)[first : first + positions]
    for d in range(N_DEPTH):
        payload_out[d, :, 0:OWN_UNITS] = grad.astype(BF16)
        payload_out[d, :, OWN_UNITS:] = stat_ref[...]
    for i in range(cols_out.shape[0]):
        cols_out[i] = cols[:, i * 128 : (i + 1) * 128]


def joint_stats(payload_ref, top):
    positions = payload_ref.shape[1]
    lane = iota((LANES, LANES), 0)
    target = iota((LANES, LANES), 1)
    wanted = target < 2 * HEADS
    pick_top = (wanted & (lane < 16) & (lane % HEADS == target % HEADS)).astype(BF16)
    pick_total = wanted & (lane >= 16) & (lane < 32) & (lane % HEADS == target % HEADS)
    stats = [payload_ref[d, :, OWN_UNITS:] for d in range(N_DEPTH)]
    tops = [dot(stat, pick_top) for stat in stats]
    joint = jnp.maximum(jnp.maximum(tops[0], tops[1]), jnp.maximum(tops[2], tops[3]))
    total = jnp.zeros_like(joint)
    for d in range(N_DEPTH):
        total += jnp.exp(tops[d] - joint) * dot(stats[d], pick_total.astype(BF16))
    small = iota((positions, LANES), 1) < 2 * HEADS
    total = jnp.where(small, total, 1.0)
    return jnp.where(small, jnp.exp(jnp.where(small, top - joint, 0.0)) / total, 0.0)


def paired(value):
    high, low = split_pair(value)
    return jnp.where(iota(value.shape, 1) < HEADS, high, low).astype(BF16)


def spread_of(d):
    lanes = iota((LANES, OWN_UNITS), 0)
    head = iota((LANES, OWN_UNITS), 1) // WIDTH + d * OWN
    return ((lanes == head) | (lanes == head + HEADS)).astype(BF16)


def share_kernel(depth_ref, payload_ref, top_ref, pool_ref, cols_ref, send_out, scale_out):
    positions = top_ref.shape[0]
    quarter = positions // N_DEPTH
    scale = joint_stats(payload_ref, top_ref[...])
    scale_out[...] = scale
    pair = paired(scale)
    row = iota((OWN_UNITS, OWN_UNITS), 0)
    column = iota((OWN_UNITS, OWN_UNITS), 1)
    source = ((column % 128) // 8) * 16 + (column // 128) * 8 + column % 8
    order = (row == source).astype(BF16)
    lane = iota((positions, LANES), 1)
    totals = jnp.zeros((positions, LANES), F32)
    for d in range(N_DEPTH):
        part = pool_ref[:, d * OWN_UNITS : (d + 1) * OWN_UNITS] * dot(pair, spread_of(d))
        product = payload_ref[d, :, 0:OWN_UNITS].astype(F32) * part
        for i in range(OWN):
            span = slice(i * WIDTH, (i + 1) * WIDTH)
            total = jnp.sum(product[:, span], axis=1, keepdims=True)
            totals = jnp.where(lane == d * OWN + i, total, totals)
        part = dot(part.astype(BF16), order).astype(BF16)
        for peer in range(8):
            xlo = peer // 4
            send_out[8 * d + peer, 0:positions, :] = part[:, xlo * 128 : (xlo + 1) * 128]
    same = (iota((positions, LANES), 0) == iota((positions, LANES), 1)).astype(BF16)
    other = (iota((positions, LANES), 0) + positions == iota((positions, LANES), 1)).astype(BF16)
    high, low = split_pair(totals)
    turned = dot(high.astype(BF16), same, 0, 0) + dot(low.astype(BF16), other, 0, 0)
    extra = [turned[0:HEADS], None, jnp.zeros((4, LANES), F32)]
    own = pl.multiple_of(depth_ref[0] * quarter, quarter)
    for peer in range(4):
        rim = cols_ref[peer, positions : positions + 16, :].astype(F32)
        extra[1] = rim[0:4]
        rest = jnp.concatenate(extra, axis=0).astype(BF16)
        local = cols_ref[peer, pl.ds(own, quarter), :]
        for block in range(2 * N_DEPTH):
            index = 4 * block + peer
            send_out[index, positions : positions + quarter, :] = local
            send_out[index, positions + quarter :, :] = rest


def gradient_kernel(
    core_ref,
    payload_ref,
    scale_ref,
    features_hbm,
    slope_hbm,
    values_hbm,
    pair_hbm,
    mine_out,
    theirs_out,
    probs_hbm,
    total,
    slope_buf,
    values_buf,
    features_buf,
    grad_buf,
    scaled_buf,
    prob_buf,
    pair_buf,
    weights_buf,
    sems,
):
    positions = scale_ref.shape[0]
    rows = features_buf.shape[0]
    reads = rows // positions
    copies = [pltpu.make_async_copy(features_hbm, features_buf, sems.at[0])]
    for d in range(N_DEPTH):
        for k, (ref, buf) in enumerate(((slope_hbm, slope_buf), (values_hbm, values_buf))):
            copies.append(pltpu.make_async_copy(ref.at[d], buf.at[d], sems.at[1 + 2 * d + k]))
    copies.append(pltpu.make_async_copy(pair_hbm, pair_buf, sems.at[1 + 2 * N_DEPTH]))
    for i in [1, 0] + list(range(2, len(copies))):
        copies[i].start()
    pair = paired(scale_ref[...])
    first = core_ref[0] == 0

    def by_read(buf, p):
        shape = (16, OWN_UNITS)
        return jnp.broadcast_to(buf[p : p + 1, :], shape).astype(BF16)[None]

    split = (reads // 16, 16, OWN_UNITS)

    def multiply(buf, d, factor):
        for p in range(positions):
            span = slice(p * reads, (p + 1) * reads)
            term = buf[d, span, :].reshape(split) * by_read(factor, p)
            buf[d, span, :] = term.reshape(reads, OWN_UNITS)

    def set_factors(d):
        grad = payload_ref[d, :, 0:OWN_UNITS].astype(F32)
        grad_buf[d % 2] = grad
        scaled_buf[d % 2] = grad * dot(pair, spread_of(d))

    def pack(d):
        for peer in range(4 * d, 4 * d + 4):
            base = d * OWN_UNITS + (peer % 4) * 4
            for q in range(4):
                for t in range(2):
                    zero = total[q, pl.ds(base + t, N_Z, stride=16), :]
                    one = total[q, pl.ds(base + 2 + t, N_Z, stride=16), :]
                    span = slice(q * 32 + t * 16, q * 32 + t * 16 + 16)
                    mine_out[peer, span, :] = jnp.where(first, zero, one).astype(BF16)
                    theirs_out[peer, span, :] = jnp.where(first, one, zero).astype(BF16)

    set_factors(0)
    copies[1].wait()
    multiply(slope_buf, 0, scaled_buf.at[0])
    copies[0].wait()
    for d in range(N_DEPTH):
        cols = slice(d * OWN_UNITS, (d + 1) * OWN_UNITS)
        copies[2 + 2 * d].wait()
        if d + 1 < N_DEPTH:
            copies[3 + 2 * d].wait()
            set_factors(d + 1)
        term = dot(slope_buf[d], features_buf[...], 0, 0)
        for q in range(4):
            total[q, cols, :] = term[:, q * 128 : (q + 1) * 128]
        if d + 1 < N_DEPTH:
            multiply(slope_buf, d + 1, scaled_buf.at[(d + 1) % 2])
        multiply(values_buf, d, grad_buf.at[d % 2])
        if d:
            pack(d - 1)
        term = dot(values_buf[d], spread_of(d), 1, 1)
        if d == 0:
            prob_buf[...] = term
        else:
            prob_buf[...] += term
    copies[1 + 2 * N_DEPTH].wait()
    lane = iota((LANES, LANES), 0)
    target = iota((LANES, LANES), 1)
    both = (lane < 16) & (target < 16) & (lane % HEADS == target % HEADS)
    weights_buf[...] = dot(pair_buf[...], both.astype(BF16))
    lane = iota((reads, LANES), 1)
    for p in range(positions):
        span = slice(p * reads, (p + 1) * reads)
        probs = weights_buf[span, :] * scale_ref[p : p + 1, :]
        prob_buf[span, :] = jnp.where(lane < HEADS, probs * prob_buf[span, :], probs)
    store = pltpu.make_async_copy(prob_buf, probs_hbm, sems.at[2 + 2 * N_DEPTH])
    store.start()
    pack(N_DEPTH - 1)
    store.wait()


def gradients(core_index, payload, scale, features, *rest):
    rows, channels = features.shape
    positions = scale.shape[0]
    shape = (PLANE + 1, 128, 128)
    return pl.pallas_call(
        gradient_kernel,
        in_specs=[SMEM] + [VMEM] * 2 + [HBM] * 4,
        out_specs=[VMEM, VMEM, HBM],
        out_shape=[
            jax.ShapeDtypeStruct(shape, BF16),
            jax.ShapeDtypeStruct(shape, BF16),
            pltpu.HBM((rows, LANES), F32),
        ],
        scratch_shapes=[
            pltpu.VMEM((4, UNITS, 128), F32),
            pltpu.VMEM((N_DEPTH, rows, OWN_UNITS), BF16),
            pltpu.VMEM((N_DEPTH, rows, OWN_UNITS), BF16),
            pltpu.VMEM((rows, channels), BF16),
            pltpu.VMEM((2, positions, OWN_UNITS), F32),
            pltpu.VMEM((2, positions, OWN_UNITS), F32),
            pltpu.VMEM((rows, LANES), F32),
            pltpu.VMEM((rows, LANES), BF16),
            pltpu.VMEM((rows, LANES), F32),
            pltpu.SemaphoreType.DMA((3 + 2 * N_DEPTH,)),
        ],
        compiler_params=pltpu.CompilerParams(vmem_limit_bytes=36 * 2**20),
        cost_estimate=pl.CostEstimate(
            flops=2 * rows * UNITS * (channels + 256),
            bytes_accessed=16 * 2**20,
            transcendentals=10**4,
        ),
    )(core_index, payload, scale, *in_hbm(features, *rest))


def score_kernel(
    place_ref,
    recv_ref,
    probs_hbm,
    features_hbm,
    _held,
    theirs_out,
    score_out,
    slot,
    probs_buf,
    features_buf,
    score_buf,
    row_buf,
    sems,
):
    rows = probs_buf.shape[0]
    positions = recv_ref.shape[1] - 32
    reads = rows // positions
    load = [
        pltpu.make_async_copy(probs_hbm, probs_buf, sems.at[0]),
        pltpu.make_async_copy(features_hbm, features_buf, sems.at[1]),
    ]
    load[0].start()
    load[1].start()
    row = jnp.zeros((16, LANES), F32)
    for d in range(N_DEPTH):
        row += recv_ref[8 * d + place_ref[0], positions + 16 : positions + 32, :].astype(F32)
    high, low = split_pair(row)
    pick = iota((16, LANES), 0) == iota((16, LANES), 1)
    pick = (pick & (iota((16, LANES), 0) < HEADS)).astype(BF16)
    turned = dot(high.astype(BF16), pick, 0, 0) + dot(low.astype(BF16), pick, 0, 0)
    row_buf[...] = turned[0:positions] + turned[positions : 2 * positions]
    load[0].wait()
    for p in range(positions):
        span = slice(p * reads, (p + 1) * reads)
        term = probs_buf[span, :]
        probs = pltpu.roll(term, LANES - HEADS, 1)
        score_buf[span, :] = (term - probs * row_buf[p : p + 1, :]).astype(BF16)
    load[1].wait()
    score = dot(score_buf[...], features_buf[...], 0, 0)[0:HEADS]
    score = [score[:, q * 128 : (q + 1) * 128] for q in range(4)]
    score = jnp.concatenate(score + [jnp.zeros((96, 128), F32)], axis=0).astype(BF16)
    slot[...] = score
    score_out[...] = score
    copy = pltpu.make_async_copy(slot, theirs_out.at[PLANE], sems.at[2])
    copy.start()
    copy.wait()


def scores(place, recv, probs, features, theirs):
    rows, channels = features.shape
    positions = recv.shape[1] - 32
    return pl.pallas_call(
        score_kernel,
        in_specs=[SMEM, VMEM, HBM, HBM, ANY],
        out_specs=[ANY, VMEM],
        out_shape=[
            jax.ShapeDtypeStruct(theirs.shape, BF16),
            jax.ShapeDtypeStruct((128, 128), BF16),
        ],
        input_output_aliases={4: 0},
        scratch_shapes=[
            pltpu.VMEM((128, 128), BF16),
            pltpu.VMEM((rows, LANES), F32),
            pltpu.VMEM((rows, channels), BF16),
            pltpu.VMEM((rows, LANES), BF16),
            pltpu.VMEM((positions, LANES), F32),
            pltpu.SemaphoreType.DMA((3,)),
        ],
        compiler_params=pltpu.CompilerParams(vmem_limit_bytes=16 * 2**20),
        cost_estimate=pl.CostEstimate(flops=10**8, bytes_accessed=10**6, transcendentals=0),
    )(place, recv, *in_hbm(probs, features), theirs)


def pair_kernel(mine_ref, score_ref, theirs_ref, send_out):
    score = score_ref[0:32, :].astype(F32) + theirs_ref[PLANE, 0:32, :].astype(F32)
    score = score.astype(BF16)
    for peer in range(PLANE):
        value = mine_ref[peer].astype(F32) + theirs_ref[peer].astype(F32)
        send_out[peer, 0:128, :] = value.astype(BF16)
        send_out[peer, 128:160, :] = score


def conv_kernel(recv_ref, part_out):
    positions = recv_ref.shape[1] - 32
    taps = part_out.shape[1] // 8
    half = taps // 2
    left, grads = [], []
    for j in range(8):
        pooled = recv_ref[j, 0:positions, :].astype(F32)
        local = [recv_ref[j, positions : positions + 16, :]]
        for d in range(1, N_DEPTH):
            pooled += recv_ref[8 * d + j, 0:positions, :].astype(F32)
            local.append(recv_ref[8 * d + j, positions : positions + 16, :])
        left.append(pooled.astype(BF16))
        rest = recv_ref[j, positions + 16 : positions + 32, :].astype(F32)
        low, high = rest[8 : 8 + half], rest[8 + half : 8 + 2 * half]
        grads.append(jnp.concatenate([low] + [x.astype(F32) for x in local] + [high], axis=0))
    left = jnp.concatenate(left, axis=0)
    for k in range(taps):
        first = 2 * half - k
        shifted = jnp.concatenate([grad[first : first + positions] for grad in grads], axis=0)
        part = dot(left, shifted.astype(BF16), 0, 0)
        part_out[:, k * 8 : (k + 1) * 8, :] = part.reshape(N_Z, 8, 128)


def line_kernel(recv_ref, conv_ref, send_out, total):
    value = recv_ref[0].astype(F32)
    for peer in range(1, PLANE):
        value += recv_ref[peer].astype(F32)
    total[...] = value
    score = value[128:160]
    for z in range(N_Z):
        block = jnp.concatenate([total[pl.ds(z, 8, stride=16), :], score, conv_ref[z]], axis=0)
        send_out[z] = block.astype(BF16)


def last_kernel(recv_ref, value_out, score_out, conv_out):
    value = recv_ref[0].astype(F32)
    for z in range(1, N_Z):
        value += recv_ref[z].astype(F32)
    for q in range(4):
        span = slice(q * 128, (q + 1) * 128)
        value_out[:, span] = value[2 * q : 2 * q + 2]
        score_out[:, span] = value[8 + 8 * q : 16 + 8 * q]
    for k in range(conv_out.shape[0]):
        conv_out[k] = value[40 + 8 * k : 48 + 8 * k]


def small_call(kernel, shapes, *operands, specs=None, scratch=(), mib=6):
    single = not isinstance(shapes, list)
    return pl.pallas_call(
        kernel,
        in_specs=specs or [VMEM] * len(operands),
        out_specs=VMEM if single else [VMEM] * len(shapes),
        out_shape=shapes,
        scratch_shapes=list(scratch),
        compiler_params=pltpu.CompilerParams(vmem_limit_bytes=mib * 2**20),
        cost_estimate=pl.CostEstimate(flops=10**6, bytes_accessed=10**5, transcendentals=0),
    )(*operands)


def exchange(block, axis):
    return lax.ppermute(block, axis, [(0, 1), (1, 0)])


def body(
    read_feats,
    base_codes,
    qual_codes,
    depth_counts,
    base_table,
    qual_table,
    value_weight,
    score_weight,
    conv_weight,
    cotangent,
):
    _, positions, reads, channels = read_feats.shape
    block_units, taps, outs = conv_weight.shape
    half = taps // 2
    depth_index = lax.axis_index("depth")
    core_index = lax.axis_index("core")
    def shaped(*shape, kind=BF16):
        return jax.ShapeDtypeStruct(shape, kind)

    count = lax.axis_size(SEQ)
    forward = [(i, i + 1) for i in range(count - 1)]
    grad_local = cotangent[0]
    low = lax.ppermute(grad_local[-half:], SEQ, forward)
    high = lax.ppermute(grad_local[:half], SEQ, [(b, a) for a, b in forward])

    features, slope, values, pair, top, stat, pool = encode(
        depth_index.reshape(1),
        depth_counts[0],
        read_feats[0],
        value_weight,
        base_codes[0].T,
        qual_codes[0].T,
        base_table,
        qual_table,
        score_weight.T,
    )

    payload, cols = small_call(
        rim_kernel,
        [shaped(N_DEPTH, positions, OWN_UNITS + LANES), shaped(4, RIM, 128)],
        low,
        grad_local,
        high,
        conv_weight.transpose(1, 0, 2),
        stat,
    )
    payload = lax.all_to_all(payload, "depth", split_axis=0, concat_axis=0, tiled=True)

    send, scale = small_call(
        share_kernel,
        [
            shaped(8 * N_DEPTH, positions + 32, 128),
            shaped(positions, LANES, kind=F32),
        ],
        depth_index.reshape(1),
        payload,
        top,
        pool,
        cols,
        specs=[SMEM] + [VMEM] * 4,
    )
    recv = lax.all_to_all(
        send, ("depth", "xlo", "xhi", "core"), split_axis=0, concat_axis=0, tiled=True
    )

    mine, theirs, probs = gradients(
        core_index.reshape(1), payload, scale, features, slope, values, pair
    )
    place = lax.axis_index(("xlo", "xhi", "core")).reshape(1)
    theirs, score = scores(place, recv, probs, features, theirs)
    theirs = exchange(theirs, "core")
    plane_send = small_call(pair_kernel, shaped(PLANE, 160, 128), mine, score, theirs)
    plane_recv = lax.all_to_all(
        plane_send, ("depth", "xlo", "xhi"), split_axis=0, concat_axis=0, tiled=True
    )
    conv_part = small_call(conv_kernel, shaped(N_Z, 8 * taps, 128, kind=F32), recv)

    line_send = small_call(
        line_kernel,
        shaped(N_Z, 40 + 8 * taps, 128),
        plane_recv,
        conv_part,
        scratch=[pltpu.VMEM((160, 128), F32)],
    )
    line_recv = lax.all_to_all(line_send, "z", split_axis=0, concat_axis=0, tiled=True)
    value_weight_grad, score_weight_grad, conv_weight_grad = small_call(
        last_kernel,
        [
            shaped(2, channels, kind=F32),
            shaped(HEADS, channels, kind=F32),
            shaped(taps, 8, 128, kind=F32),
        ],
        line_recv,
    )
    return (value_weight_grad, score_weight_grad.T, conv_weight_grad.transpose(1, 0, 2))


def solution(mesh):
    fine = Mesh(mesh.devices.reshape(N_DEPTH, N_Z, 2, 2, 2), AXES)
    rep = ("xhi", "core")
    placed = (
        P(rep, SEQ, "depth", None),
        P(rep, SEQ, "depth"),
        P(rep, SEQ, "depth"),
        P(rep, SEQ),
        P(),
        P(),
        P(),
        P(),
        P("depth", None, None),
        P(rep, SEQ, None),
    )
    return jax.shard_map(
        body,
        mesh=fine,
        in_specs=placed,
        out_specs=(P(AXES, None), P(), P(("depth",) + SEQ, None, rep)),
        check_vma=False,
    )
```

```python
import jax
import jax.numpy as jnp
from jax import lax
from jax.experimental import pallas as pl
from jax.experimental.pallas import tpu as pltpu
from jax.sharding import Mesh, PartitionSpec as P

AXES = ("depth", "z", "xlo", "xhi", "core")
SEQ = ("z", "xlo")
F32 = jnp.float32
BF16 = jnp.bfloat16
I32 = jnp.int32

TILE = 16
LANES = 128
HEADS = 8
WIDTH = 128
OWN = 2
OWN_UNITS = OWN * WIDTH
UNITS = HEADS * WIDTH
RIM = 80
N_DEPTH = 4
N_Z = 16
PLANE = 16


def iota(shape, dim):
    return lax.broadcasted_iota(I32, shape, dim)


def dot(a, b, ca=1, cb=0):
    return lax.dot_general(a, b, (((ca,), (cb,)), ((), ())), preferred_element_type=F32)


def split_pair(value):
    high = value.astype(BF16).astype(F32)
    return high, value - high


def encode_kernel(
    depth_ref,
    count_ref,
    feat_hbm,
    base_codes_ref,
    qual_codes_ref,
    base_ref,
    qual_ref,
    score_ref,
    features_out,
    pair_out,
    top_out,
    stat_out,
    feat_buf,
    features_buf,
    hot_buf,
    embed_buf,
    score_buf,
    stat_buf,
    sems,
    out_sems,
):
    positions, reads, channels = feat_buf.shape
    tiles = positions // TILE
    rows = TILE * reads
    copies = []
    for i in range(tiles):
        span = pl.ds(i * TILE, TILE)
        copies.append(pltpu.make_async_copy(feat_hbm.at[span], feat_buf.at[span], sems.at[i]))
        copies[i].start()
    stores = []
    n_qual, n_base = qual_ref.shape[0], base_ref.shape[0]
    place = (iota((LANES, n_qual), 0) == iota((LANES, n_qual), 1)).astype(BF16)
    table = dot(place, qual_ref[...])
    place = (iota((LANES, n_base), 0) == iota((LANES, n_base), 1) + 96).astype(BF16)
    table = (table + dot(place, base_ref[...])).astype(BF16)
    slot = iota((LANES, HEADS), 0)
    place = (slot % HEADS == iota((LANES, HEADS), 1)) & (slot < 4 * HEADS)
    score_weight = dot(place.astype(BF16), score_ref[...]).astype(BF16)
    lane = iota((reads, LANES), 1)
    read = iota((reads, LANES), 0) + depth_ref[0] * reads
    for i in range(tiles):
        first_row = i * rows
        for p in range(TILE):
            at = i * TILE + p
            qual = jnp.broadcast_to(qual_codes_ref[:, at : at + 1], (reads, LANES))
            base = jnp.broadcast_to(base_codes_ref[:, at : at + 1], (reads, LANES))
            hot = (lane == qual) | (lane == base + 96)
            hot_buf[p * reads : (p + 1) * reads, :] = hot.astype(BF16)
        embed_buf[...] = dot(hot_buf[...], table)
        copies[i].wait()
        for p in range(TILE):
            near = slice(p * reads, (p + 1) * reads)
            feature = feat_buf[i * TILE + p].astype(F32) + embed_buf[near, :]
            far = slice(first_row + p * reads, first_row + (p + 1) * reads)
            features_buf[far, :] = feature.astype(BF16)
        at = pl.ds(first_row, rows)
        stores.append(
            pltpu.make_async_copy(features_buf.at[at], features_out.at[at], out_sems.at[i])
        )
        stores[i].start()
    features = features_buf[...]
    score_buf[...] = dot(features, score_weight, 1, 1)
    for p in range(positions):
        near = slice(p * reads, (p + 1) * reads)
        scores = score_buf[near, :]
        live = read < count_ref[p]
        top = jnp.max(jnp.where(live, scores, -1e30), axis=0, keepdims=True)
        top_high, top_rest = split_pair(top)
        top_low = top_rest.astype(BF16).astype(F32)
        top = top_high + top_low
        weights = jnp.where(live, jnp.exp(scores - top), 0.0)
        total_high, total_low = split_pair(jnp.sum(weights, axis=0, keepdims=True))
        small = lane[0:1]
        stat_buf[p : p + 1, :] = jnp.where(
            small < 8,
            top_high,
            jnp.where(small < 16, top_low, jnp.where(small < 24, total_high, total_low)),
        )
        top_out[p : p + 1, :] = top
        high, low = split_pair(weights)
        pair_out[near, :] = jnp.where(lane < HEADS, high, low).astype(BF16)
    stat_out[...] = stat_buf[...].astype(BF16)
    for store in stores:
        store.wait()


def value_kernel(
    pair_ref,
    features_hbm,
    value_hbm,
    pair_out,
    slope_out,
    values_out,
    pool_out,
    features_buf,
    value_buf,
    slope_buf,
    values_buf,
    preact_buf,
    spread_buf,
    load_sems,
    sems,
):
    positions = pool_out.shape[0]
    reads = features_buf.shape[0] // positions
    load = [
        pltpu.make_async_copy(features_hbm, features_buf, load_sems.at[0]),
        pltpu.make_async_copy(value_hbm, value_buf, load_sems.at[1]),
    ]
    for copy in load:
        copy.start()
    spread_buf[0] = dot(pair_ref[...], spread_of(0))
    for copy in load:
        copy.wait()
    stores = [pltpu.make_async_copy(pair_ref, pair_out, sems.at[1])]
    stores[0].start()

    def multiply(part):
        cols = slice(part * OWN_UNITS, (part + 1) * OWN_UNITS)
        preact_buf[part % 2] = dot(features_buf[...], value_buf[cols, :], 1, 1)
        if part:
            spread_buf[part % 2] = dot(pair_ref[...], spread_of(part))

    multiply(0)
    for part in range(N_DEPTH):
        if part + 1 < N_DEPTH:
            multiply(part + 1)
        cols = slice(part * OWN_UNITS, (part + 1) * OWN_UNITS)
        for p in range(positions):
            near = slice(p * reads, (p + 1) * reads)
            preact = preact_buf[part % 2, near, :].astype(BF16)
            spread = spread_buf[part % 2, near, :].astype(BF16)
            sigma = 0.5 * jnp.tanh(0.5 * preact) + 0.5
            values = preact * sigma
            slope = sigma + values * (1.0 - sigma)
            slope_buf[part, near, :] = spread * slope
            values_buf[part, near, :] = values
            pool = jnp.sum((spread * values).astype(F32), axis=0, keepdims=True)
            pool_out[p : p + 1, cols] = pool
            if (p + 1) % (positions // 2) == 0:
                side = (p + 1) // (positions // 2) - 1
                at = pl.ds(side * (positions // 2) * reads, positions // 2 * reads)
                pairs = ((slope_buf, slope_out), (values_buf, values_out))
                for k, (buf, out) in enumerate(pairs):
                    sem = sems.at[2 + 4 * part + 2 * side + k]
                    stores.append(pltpu.make_async_copy(buf.at[part, at], out.at[part, at], sem))
                    stores[-1].start()
    for store in stores:
        store.wait()


VMEM = pl.BlockSpec(memory_space=pltpu.VMEM)
SMEM = pl.BlockSpec(memory_space=pltpu.SMEM)
HBM = pl.BlockSpec(memory_space=pltpu.HBM)
ANY = pl.BlockSpec(memory_space=pl.ANY)


def in_hbm(*arrays):
    return [pltpu.with_memory_space_constraint(array, pltpu.HBM) for array in arrays]


def encode(depth_index, counts, feats, *rest):
    positions, reads, channels = feats.shape
    rows = positions * reads
    step = TILE * reads
    return pl.pallas_call(
        encode_kernel,
        in_specs=[SMEM, SMEM, HBM] + [VMEM] * 5,
        out_specs=[HBM] + [VMEM] * 3,
        out_shape=[
            pltpu.HBM((rows, channels), BF16),
            jax.ShapeDtypeStruct((rows, LANES), BF16),
            jax.ShapeDtypeStruct((positions, LANES), F32),
            jax.ShapeDtypeStruct((positions, LANES), BF16),
        ],
        scratch_shapes=[
            pltpu.VMEM(feats.shape, BF16),
            pltpu.VMEM((rows, channels), BF16),
            pltpu.VMEM((step, LANES), BF16),
            pltpu.VMEM((step, channels), F32),
            pltpu.VMEM((rows, LANES), F32),
            pltpu.VMEM((positions, LANES), F32),
            pltpu.SemaphoreType.DMA((positions // TILE,)),
            pltpu.SemaphoreType.DMA((positions // TILE,)),
        ],
        compiler_params=pltpu.CompilerParams(vmem_limit_bytes=20 * 2**20),
        cost_estimate=pl.CostEstimate(
            flops=2 * rows * channels * 256, bytes_accessed=4 * 2**20, transcendentals=rows * LANES
        ),
    )(depth_index, *in_hbm(counts, feats, *rest))


def make_values(features, pair, value_weight, positions):
    rows, channels = features.shape
    return pl.pallas_call(
        value_kernel,
        in_specs=[VMEM, HBM, HBM],
        out_specs=[HBM] * 3 + [VMEM],
        out_shape=[
            pltpu.HBM((rows, LANES), BF16),
            pltpu.HBM((N_DEPTH, rows, OWN_UNITS), BF16),
            pltpu.HBM((N_DEPTH, rows, OWN_UNITS), BF16),
            jax.ShapeDtypeStruct((positions, UNITS), F32),
        ],
        scratch_shapes=[
            pltpu.VMEM((rows, channels), BF16),
            pltpu.VMEM(value_weight.shape, BF16),
            pltpu.VMEM((N_DEPTH, rows, OWN_UNITS), BF16),
            pltpu.VMEM((N_DEPTH, rows, OWN_UNITS), BF16),
            pltpu.VMEM((2, rows, OWN_UNITS), F32),
            pltpu.VMEM((2, rows, OWN_UNITS), F32),
            pltpu.SemaphoreType.DMA((2,)),
            pltpu.SemaphoreType.DMA((2 + 4 * N_DEPTH,)),
        ],
        compiler_params=pltpu.CompilerParams(vmem_limit_bytes=32 * 2**20),
        cost_estimate=pl.CostEstimate(
            flops=2 * rows * UNITS * (channels + 256),
            bytes_accessed=16 * 2**20,
            transcendentals=rows * UNITS,
        ),
    )(pair, *in_hbm(features, value_weight))


def rim_kernel(before_ref, local_ref, after_ref, weight_ref, stat_ref, payload_out, cols_out):
    positions, outs = local_ref.shape
    taps = weight_ref.shape[0]
    half = taps // 2
    rows = cols_out.shape[1]
    low = before_ref[positions - 16 :, :].astype(F32)[16 - half :]
    high = after_ref[0:16, :].astype(F32)[:half]
    local = local_ref[...].astype(F32)
    pad = jnp.zeros((rows - positions - 2 * half, outs), F32)
    rim = jnp.concatenate([low, local, high, pad], axis=0).astype(BF16)
    cols = jnp.concatenate([local, low, high, pad], axis=0).astype(BF16)
    grad = jnp.zeros((positions, OWN_UNITS), F32)
    for k in range(taps):
        first = 2 * half - k
        grad += dot(rim, weight_ref[k], 1, 1)[first : first + positions]
    for d in range(N_DEPTH):
        payload_out[d, :, 0:OWN_UNITS] = grad.astype(BF16)
        payload_out[d, :, OWN_UNITS:] = stat_ref[...]
    for i in range(cols_out.shape[0]):
        cols_out[i] = cols[:, i * 128 : (i + 1) * 128]


def joint_stats(payload_ref, top):
    positions = payload_ref.shape[1]
    lane = iota((LANES, LANES), 0)
    target = iota((LANES, LANES), 1)
    wanted = target < 2 * HEADS
    pick_top = (wanted & (lane < 16) & (lane % HEADS == target % HEADS)).astype(BF16)
    pick_total = wanted & (lane >= 16) & (lane < 32) & (lane % HEADS == target % HEADS)
    stats = [payload_ref[d, :, OWN_UNITS:] for d in range(N_DEPTH)]
    tops = [dot(stat, pick_top) for stat in stats]
    joint = jnp.maximum(jnp.maximum(tops[0], tops[1]), jnp.maximum(tops[2], tops[3]))
    total = jnp.zeros_like(joint)
    for d in range(N_DEPTH):
        total += jnp.exp(tops[d] - joint) * dot(stats[d], pick_total.astype(BF16))
    small = iota((positions, LANES), 1) < 2 * HEADS
    total = jnp.where(small, total, 1.0)
    return jnp.where(small, jnp.exp(jnp.where(small, top - joint, 0.0)) / total, 0.0)


def paired(value):
    high, low = split_pair(value)
    return jnp.where(iota(value.shape, 1) < HEADS, high, low).astype(BF16)


def spread_of(d):
    lanes = iota((LANES, OWN_UNITS), 0)
    head = iota((LANES, OWN_UNITS), 1) // WIDTH + d * OWN
    return ((lanes == head) | (lanes == head + HEADS)).astype(BF16)


def share_kernel(depth_ref, payload_ref, top_ref, pool_ref, cols_ref, send_out, scale_out):
    positions = top_ref.shape[0]
    quarter = positions // N_DEPTH
    scale = joint_stats(payload_ref, top_ref[...])
    scale_out[...] = scale
    pair = paired(scale)
    row = iota((OWN_UNITS, OWN_UNITS), 0)
    column = iota((OWN_UNITS, OWN_UNITS), 1)
    source = ((column % 128) // 8) * 16 + (column // 128) * 8 + column % 8
    order = (row == source).astype(BF16)
    lane = iota((positions, LANES), 1)
    totals = jnp.zeros((positions, LANES), F32)
    for d in range(N_DEPTH):
        part = pool_ref[:, d * OWN_UNITS : (d + 1) * OWN_UNITS] * dot(pair, spread_of(d))
        product = payload_ref[d, :, 0:OWN_UNITS].astype(F32) * part
        for i in range(OWN):
            span = slice(i * WIDTH, (i + 1) * WIDTH)
            total = jnp.sum(product[:, span], axis=1, keepdims=True)
            totals = jnp.where(lane == d * OWN + i, total, totals)
        part = dot(part.astype(BF16), order).astype(BF16)
        for peer in range(8):
            xlo = peer // 4
            send_out[8 * d + peer, 0:positions, :] = part[:, xlo * 128 : (xlo + 1) * 128]
    same = (iota((positions, LANES), 0) == iota((positions, LANES), 1)).astype(BF16)
    other = (iota((positions, LANES), 0) + positions == iota((positions, LANES), 1)).astype(BF16)
    high, low = split_pair(totals)
    turned = dot(high.astype(BF16), same, 0, 0) + dot(low.astype(BF16), other, 0, 0)
    extra = [turned[0:HEADS], None, jnp.zeros((4, LANES), F32)]
    own = pl.multiple_of(depth_ref[0] * quarter, quarter)
    for peer in range(4):
        rim = cols_ref[peer, positions : positions + 16, :].astype(F32)
        extra[1] = rim[0:4]
        rest = jnp.concatenate(extra, axis=0).astype(BF16)
        local = cols_ref[peer, pl.ds(own, quarter), :]
        for block in range(2 * N_DEPTH):
            index = 4 * block + peer
            send_out[index, positions : positions + quarter, :] = local
            send_out[index, positions + quarter :, :] = rest


def gradient_kernel(
    core_ref,
    payload_ref,
    scale_ref,
    features_hbm,
    slope_hbm,
    values_hbm,
    pair_hbm,
    mine_out,
    theirs_out,
    probs_hbm,
    total,
    slope_buf,
    values_buf,
    features_buf,
    grad_buf,
    scaled_buf,
    prob_buf,
    pair_buf,
    weights_buf,
    sems,
):
    positions = scale_ref.shape[0]
    rows = features_buf.shape[0]
    reads = rows // positions
    copies = [pltpu.make_async_copy(features_hbm, features_buf, sems.at[0])]
    for d in range(N_DEPTH):
        for k, (ref, buf) in enumerate(((slope_hbm, slope_buf), (values_hbm, values_buf))):
            copies.append(pltpu.make_async_copy(ref.at[d], buf.at[d], sems.at[1 + 2 * d + k]))
    copies.append(pltpu.make_async_copy(pair_hbm, pair_buf, sems.at[1 + 2 * N_DEPTH]))
    for i in [1, 0] + list(range(2, len(copies))):
        copies[i].start()
    pair = paired(scale_ref[...])
    first = core_ref[0] == 0

    def by_read(buf, p):
        shape = (16, OWN_UNITS)
        return jnp.broadcast_to(buf[p : p + 1, :], shape).astype(BF16)[None]

    split = (reads // 16, 16, OWN_UNITS)

    def multiply(buf, d, factor):
        for p in range(positions):
            span = slice(p * reads, (p + 1) * reads)
            term = buf[d, span, :].reshape(split) * by_read(factor, p)
            buf[d, span, :] = term.reshape(reads, OWN_UNITS)

    def set_factors(d):
        grad = payload_ref[d, :, 0:OWN_UNITS].astype(F32)
        grad_buf[d % 2] = grad
        scaled_buf[d % 2] = grad * dot(pair, spread_of(d))

    def pack(d):
        for peer in range(4 * d, 4 * d + 4):
            base = d * OWN_UNITS + (peer % 4) * 4
            for q in range(4):
                for t in range(2):
                    zero = total[q, pl.ds(base + t, N_Z, stride=16), :]
                    one = total[q, pl.ds(base + 2 + t, N_Z, stride=16), :]
                    span = slice(q * 32 + t * 16, q * 32 + t * 16 + 16)
                    mine_out[peer, span, :] = jnp.where(first, zero, one).astype(BF16)
                    theirs_out[peer, span, :] = jnp.where(first, one, zero).astype(BF16)

    set_factors(0)
    copies[1].wait()
    multiply(slope_buf, 0, scaled_buf.at[0])
    copies[0].wait()
    for d in range(N_DEPTH):
        cols = slice(d * OWN_UNITS, (d + 1) * OWN_UNITS)
        copies[2 + 2 * d].wait()
        if d + 1 < N_DEPTH:
            copies[3 + 2 * d].wait()
            set_factors(d + 1)
        term = dot(slope_buf[d], features_buf[...], 0, 0)
        for q in range(4):
            total[q, cols, :] = term[:, q * 128 : (q + 1) * 128]
        if d + 1 < N_DEPTH:
            multiply(slope_buf, d + 1, scaled_buf.at[(d + 1) % 2])
        multiply(values_buf, d, grad_buf.at[d % 2])
        if d:
            pack(d - 1)
        term = dot(values_buf[d], spread_of(d), 1, 1)
        if d == 0:
            prob_buf[...] = term
        else:
            prob_buf[...] += term
    copies[1 + 2 * N_DEPTH].wait()
    lane = iota((LANES, LANES), 0)
    target = iota((LANES, LANES), 1)
    both = (lane < 16) & (target < 16) & (lane % HEADS == target % HEADS)
    weights_buf[...] = dot(pair_buf[...], both.astype(BF16))
    lane = iota((reads, LANES), 1)
    for p in range(positions):
        span = slice(p * reads, (p + 1) * reads)
        probs = weights_buf[span, :] * scale_ref[p : p + 1, :]
        prob_buf[span, :] = jnp.where(lane < HEADS, probs * prob_buf[span, :], probs)
    store = pltpu.make_async_copy(prob_buf, probs_hbm, sems.at[2 + 2 * N_DEPTH])
    store.start()
    pack(N_DEPTH - 1)
    store.wait()


def gradients(core_index, payload, scale, features, *rest):
    rows, channels = features.shape
    positions = scale.shape[0]
    shape = (PLANE, 128, 128)
    return pl.pallas_call(
        gradient_kernel,
        in_specs=[SMEM] + [VMEM] * 2 + [HBM] * 4,
        out_specs=[VMEM, VMEM, HBM],
        out_shape=[
            jax.ShapeDtypeStruct(shape, BF16),
            jax.ShapeDtypeStruct(shape, BF16),
            pltpu.HBM((rows, LANES), F32),
        ],
        scratch_shapes=[
            pltpu.VMEM((4, UNITS, 128), F32),
            pltpu.VMEM((N_DEPTH, rows, OWN_UNITS), BF16),
            pltpu.VMEM((N_DEPTH, rows, OWN_UNITS), BF16),
            pltpu.VMEM((rows, channels), BF16),
            pltpu.VMEM((2, positions, OWN_UNITS), F32),
            pltpu.VMEM((2, positions, OWN_UNITS), F32),
            pltpu.VMEM((rows, LANES), F32),
            pltpu.VMEM((rows, LANES), BF16),
            pltpu.VMEM((rows, LANES), F32),
            pltpu.SemaphoreType.DMA((3 + 2 * N_DEPTH,)),
        ],
        compiler_params=pltpu.CompilerParams(vmem_limit_bytes=36 * 2**20),
        cost_estimate=pl.CostEstimate(
            flops=2 * rows * UNITS * (channels + 256),
            bytes_accessed=16 * 2**20,
            transcendentals=10**4,
        ),
    )(core_index, payload, scale, *in_hbm(features, *rest))


def score_kernel(
    place_ref,
    recv_ref,
    probs_hbm,
    features_hbm,
    score_out,
    probs_buf,
    features_buf,
    score_buf,
    row_buf,
    sems,
):
    rows = probs_buf.shape[0]
    positions = recv_ref.shape[1] - 32
    reads = rows // positions
    load = [
        pltpu.make_async_copy(probs_hbm, probs_buf, sems.at[0]),
        pltpu.make_async_copy(features_hbm, features_buf, sems.at[1]),
    ]
    load[0].start()
    load[1].start()
    row = jnp.zeros((16, LANES), F32)
    for d in range(N_DEPTH):
        row += recv_ref[8 * d + place_ref[0], positions + 16 : positions + 32, :].astype(F32)
    high, low = split_pair(row)
    pick = iota((16, LANES), 0) == iota((16, LANES), 1)
    pick = (pick & (iota((16, LANES), 0) < HEADS)).astype(BF16)
    turned = dot(high.astype(BF16), pick, 0, 0) + dot(low.astype(BF16), pick, 0, 0)
    row_buf[...] = turned[0:positions] + turned[positions : 2 * positions]
    load[0].wait()
    for p in range(positions):
        span = slice(p * reads, (p + 1) * reads)
        term = probs_buf[span, :]
        probs = pltpu.roll(term, LANES - HEADS, 1)
        score_buf[span, :] = (term - probs * row_buf[p : p + 1, :]).astype(BF16)
    load[1].wait()
    score = dot(score_buf[...], features_buf[...], 0, 0)[0:HEADS]
    score = [score[:, q * 128 : (q + 1) * 128] for q in range(4)]
    score_out[...] = jnp.concatenate(score, axis=0).astype(BF16)


def scores(place, recv, probs, features):
    rows, channels = features.shape
    positions = recv.shape[1] - 32
    return pl.pallas_call(
        score_kernel,
        in_specs=[SMEM, VMEM, HBM, HBM],
        out_specs=VMEM,
        out_shape=jax.ShapeDtypeStruct((4 * HEADS, 128), BF16),
        scratch_shapes=[
            pltpu.VMEM((rows, LANES), F32),
            pltpu.VMEM((rows, channels), BF16),
            pltpu.VMEM((rows, LANES), BF16),
            pltpu.VMEM((positions, LANES), F32),
            pltpu.SemaphoreType.DMA((2,)),
        ],
        compiler_params=pltpu.CompilerParams(vmem_limit_bytes=16 * 2**20),
        cost_estimate=pl.CostEstimate(flops=10**8, bytes_accessed=10**6, transcendentals=0),
    )(place, recv, *in_hbm(probs, features))


def pair_kernel(mine_ref, theirs_ref, score_ref, other_ref, send_out):
    score = score_ref[...].astype(F32) + other_ref[...].astype(F32)
    score = score.astype(BF16)
    for peer in range(PLANE):
        value = mine_ref[peer].astype(F32) + theirs_ref[peer].astype(F32)
        send_out[peer, 0:128, :] = value.astype(BF16)
        send_out[peer, 128:160, :] = score


def conv_kernel(recv_ref, part_out):
    positions = recv_ref.shape[1] - 32
    taps = part_out.shape[1] // 8
    half = taps // 2
    left, grads = [], []
    for j in range(8):
        pooled = recv_ref[j, 0:positions, :].astype(F32)
        local = [recv_ref[j, positions : positions + 16, :]]
        for d in range(1, N_DEPTH):
            pooled += recv_ref[8 * d + j, 0:positions, :].astype(F32)
            local.append(recv_ref[8 * d + j, positions : positions + 16, :])
        left.append(pooled.astype(BF16))
        rest = recv_ref[j, positions + 16 : positions + 32, :].astype(F32)
        low, high = rest[8 : 8 + half], rest[8 + half : 8 + 2 * half]
        grads.append(jnp.concatenate([low] + [x.astype(F32) for x in local] + [high], axis=0))
    left = jnp.concatenate(left, axis=0)
    for k in range(taps):
        first = 2 * half - k
        shifted = jnp.concatenate([grad[first : first + positions] for grad in grads], axis=0)
        part = dot(left, shifted.astype(BF16), 0, 0)
        part_out[:, k * 8 : (k + 1) * 8, :] = part.reshape(N_Z, 8, 128)


def line_kernel(recv_ref, conv_ref, send_out, total):
    value = recv_ref[0].astype(F32)
    for peer in range(1, PLANE):
        value += recv_ref[peer].astype(F32)
    total[...] = value
    score = value[128:160]
    for z in range(N_Z):
        block = jnp.concatenate([total[pl.ds(z, 8, stride=16), :], score, conv_ref[z]], axis=0)
        send_out[z] = block.astype(BF16)


def last_kernel(recv_ref, value_out, score_out, conv_out):
    value = recv_ref[0].astype(F32)
    for z in range(1, N_Z):
        value += recv_ref[z].astype(F32)
    for q in range(4):
        span = slice(q * 128, (q + 1) * 128)
        value_out[:, span] = value[2 * q : 2 * q + 2]
        score_out[:, span] = value[8 + 8 * q : 16 + 8 * q]
    for k in range(conv_out.shape[0]):
        conv_out[k] = value[40 + 8 * k : 48 + 8 * k]


def small_call(kernel, shapes, *operands, specs=None, scratch=(), mib=6):
    single = not isinstance(shapes, list)
    return pl.pallas_call(
        kernel,
        in_specs=specs or [VMEM] * len(operands),
        out_specs=VMEM if single else [VMEM] * len(shapes),
        out_shape=shapes,
        scratch_shapes=list(scratch),
        compiler_params=pltpu.CompilerParams(vmem_limit_bytes=mib * 2**20),
        cost_estimate=pl.CostEstimate(flops=10**6, bytes_accessed=10**5, transcendentals=0),
    )(*operands)


def exchange(block, axis):
    return lax.ppermute(block, axis, [(0, 1), (1, 0)])


def body(
    read_feats,
    base_codes,
    qual_codes,
    depth_counts,
    base_table,
    qual_table,
    value_weight,
    score_weight,
    conv_weight,
    cotangent,
):
    _, positions, reads, channels = read_feats.shape
    block_units, taps, outs = conv_weight.shape
    depth_index = lax.axis_index("depth")
    core_index = lax.axis_index("core")
    def shaped(*shape, kind=BF16):
        return jax.ShapeDtypeStruct(shape, kind)

    count = lax.axis_size(SEQ)
    forward = [(i, i + 1) for i in range(count - 1)]
    grad_local = cotangent[0]
    before = lax.ppermute(grad_local, SEQ, forward)
    after = lax.ppermute(grad_local, SEQ, [(b, a) for a, b in forward])

    features, pair, top, stat = encode(
        depth_index.reshape(1),
        depth_counts[0],
        read_feats[0],
        base_codes[0].T,
        qual_codes[0].T,
        base_table,
        qual_table,
        score_weight.T,
    )

    payload, cols = small_call(
        rim_kernel,
        [shaped(N_DEPTH, positions, OWN_UNITS + LANES), shaped(4, RIM, 128)],
        before,
        grad_local,
        after,
        conv_weight.transpose(1, 0, 2),
        stat,
    )
    payload = lax.all_to_all(payload, "depth", split_axis=0, concat_axis=0, tiled=True)

    pair, slope, values, pool = make_values(features, pair, value_weight, positions)

    send, scale = small_call(
        share_kernel,
        [
            shaped(8 * N_DEPTH, positions + 32, 128),
            shaped(positions, LANES, kind=F32),
        ],
        depth_index.reshape(1),
        payload,
        top,
        pool,
        cols,
        specs=[SMEM] + [VMEM] * 4,
    )
    recv = lax.all_to_all(
        send, ("depth", "xlo", "xhi", "core"), split_axis=0, concat_axis=0, tiled=True
    )

    mine, theirs, probs = gradients(
        core_index.reshape(1), payload, scale, features, slope, values, pair
    )
    place = lax.axis_index(("xlo", "xhi", "core")).reshape(1)
    theirs = exchange(theirs, "core")
    score = scores(place, recv, probs, features)
    other = exchange(score, "core")
    plane_send = small_call(
        pair_kernel, shaped(PLANE, 160, 128), mine, theirs, score, other
    )
    plane_recv = lax.all_to_all(
        plane_send, ("depth", "xlo", "xhi"), split_axis=0, concat_axis=0, tiled=True
    )
    conv_part = small_call(conv_kernel, shaped(N_Z, 8 * taps, 128, kind=F32), recv)

    line_send = small_call(
        line_kernel,
        shaped(N_Z, 40 + 8 * taps, 128),
        plane_recv,
        conv_part,
        scratch=[pltpu.VMEM((160, 128), F32)],
    )
    line_recv = lax.all_to_all(line_send, "z", split_axis=0, concat_axis=0, tiled=True)
    value_weight_grad, score_weight_grad, conv_weight_grad = small_call(
        last_kernel,
        [
            shaped(2, channels, kind=F32),
            shaped(HEADS, channels, kind=F32),
            shaped(taps, 8, 128, kind=F32),
        ],
        line_recv,
    )
    return (value_weight_grad, score_weight_grad.T, conv_weight_grad.transpose(1, 0, 2))


def solution(mesh):
    fine = Mesh(mesh.devices.reshape(N_DEPTH, N_Z, 2, 2, 2), AXES)
    rep = ("xhi", "core")
    placed = (
        P(rep, SEQ, "depth", None),
        P(rep, SEQ, "depth"),
        P(rep, SEQ, "depth"),
        P(rep, SEQ),
        P(),
        P(),
        P(),
        P(),
        P("depth", None, None),
        P(rep, SEQ, None),
    )
    return jax.shard_map(
        body,
        mesh=fine,
        in_specs=placed,
        out_specs=(P(AXES, None), P(), P(("depth",) + SEQ, None, rep)),
        check_vma=False,
    )
```

```python
import jax
import jax.numpy as jnp
from jax import lax
from jax.experimental import pallas as pl
from jax.experimental.pallas import tpu as pltpu
from jax.sharding import Mesh, PartitionSpec as P

AXES = ("depth", "z", "xlo", "xhi", "core")
SEQ = ("z", "xlo")
F32 = jnp.float32
BF16 = jnp.bfloat16
I32 = jnp.int32

TILE = 16
LANES = 128
HEADS = 8
WIDTH = 128
OWN = 2
OWN_UNITS = OWN * WIDTH
UNITS = HEADS * WIDTH
RIM = 80
N_DEPTH = 4
N_Z = 16
PLANE = 16


def iota(shape, dim):
    return lax.broadcasted_iota(I32, shape, dim)


def dot(a, b, ca=1, cb=0):
    return lax.dot_general(a, b, (((ca,), (cb,)), ((), ())), preferred_element_type=F32)


def split_pair(value):
    high = value.astype(BF16).astype(F32)
    return high, value - high


def encode_kernel(
    depth_ref,
    count_ref,
    feat_hbm,
    base_codes_ref,
    qual_codes_ref,
    base_ref,
    qual_ref,
    score_ref,
    features_out,
    pair_out,
    top_out,
    stat_out,
    feat_buf,
    features_buf,
    hot_buf,
    embed_buf,
    score_buf,
    stat_buf,
    sems,
    out_sems,
):
    positions, reads, channels = feat_buf.shape
    tiles = positions // TILE
    rows = TILE * reads
    copies = []
    for i in range(tiles):
        span = pl.ds(i * TILE, TILE)
        copies.append(pltpu.make_async_copy(feat_hbm.at[span], feat_buf.at[span], sems.at[i]))
        copies[i].start()
    stores = []
    n_qual, n_base = qual_ref.shape[0], base_ref.shape[0]
    place = (iota((LANES, n_qual), 0) == iota((LANES, n_qual), 1)).astype(BF16)
    table = dot(place, qual_ref[...])
    place = (iota((LANES, n_base), 0) == iota((LANES, n_base), 1) + 96).astype(BF16)
    table = (table + dot(place, base_ref[...])).astype(BF16)
    slot = iota((LANES, HEADS), 0)
    place = (slot % HEADS == iota((LANES, HEADS), 1)) & (slot < 4 * HEADS)
    score_weight = dot(place.astype(BF16), score_ref[...]).astype(BF16)
    lane = iota((reads, LANES), 1)
    read = iota((reads, LANES), 0) + depth_ref[0] * reads
    for i in range(tiles):
        first_row = i * rows
        for p in range(TILE):
            at = i * TILE + p
            qual = jnp.broadcast_to(qual_codes_ref[:, at : at + 1], (reads, LANES))
            base = jnp.broadcast_to(base_codes_ref[:, at : at + 1], (reads, LANES))
            hot = (lane == qual) | (lane == base + 96)
            hot_buf[p * reads : (p + 1) * reads, :] = hot.astype(BF16)
        embed_buf[...] = dot(hot_buf[...], table)
        copies[i].wait()
        for p in range(TILE):
            near = slice(p * reads, (p + 1) * reads)
            feature = feat_buf[i * TILE + p].astype(F32) + embed_buf[near, :]
            far = slice(first_row + p * reads, first_row + (p + 1) * reads)
            features_buf[far, :] = feature.astype(BF16)
        at = pl.ds(first_row, rows)
        stores.append(
            pltpu.make_async_copy(features_buf.at[at], features_out.at[at], out_sems.at[i])
        )
        stores[i].start()
    features = features_buf[...]
    score_buf[...] = dot(features, score_weight, 1, 1)
    for p in range(positions):
        near = slice(p * reads, (p + 1) * reads)
        scores = score_buf[near, :]
        live = read < count_ref[p]
        top = jnp.max(jnp.where(live, scores, -1e30), axis=0, keepdims=True)
        top_high, top_rest = split_pair(top)
        top_low = top_rest.astype(BF16).astype(F32)
        top = top_high + top_low
        weights = jnp.where(live, jnp.exp(scores - top), 0.0)
        total_high, total_low = split_pair(jnp.sum(weights, axis=0, keepdims=True))
        small = lane[0:1]
        stat_buf[p : p + 1, :] = jnp.where(
            small < 8,
            top_high,
            jnp.where(small < 16, top_low, jnp.where(small < 24, total_high, total_low)),
        )
        top_out[p : p + 1, :] = top
        high, low = split_pair(weights)
        pair_out[near, :] = jnp.where(lane < HEADS, high, low).astype(BF16)
    stat_out[...] = stat_buf[...].astype(BF16)
    for store in stores:
        store.wait()


def value_kernel(
    pair_ref,
    value_ref,
    features_hbm,
    pair_out,
    slope_out,
    values_out,
    pool_out,
    features_buf,
    slope_buf,
    values_buf,
    preact_buf,
    spread_buf,
    load_sem,
    sems,
):
    positions = pool_out.shape[0]
    reads = features_buf.shape[0] // positions
    load = pltpu.make_async_copy(features_hbm, features_buf, load_sem)
    load.start()
    spread_buf[0] = dot(pair_ref[...], spread_of(0))
    load.wait()
    stores = [pltpu.make_async_copy(pair_ref, pair_out, sems.at[1])]
    stores[0].start()

    def multiply(part):
        cols = slice(part * OWN_UNITS, (part + 1) * OWN_UNITS)
        preact_buf[part % 2] = dot(features_buf[...], value_ref[cols, :], 1, 1)
        if part:
            spread_buf[part % 2] = dot(pair_ref[...], spread_of(part))

    multiply(0)
    for part in range(N_DEPTH):
        if part + 1 < N_DEPTH:
            multiply(part + 1)
        cols = slice(part * OWN_UNITS, (part + 1) * OWN_UNITS)
        for p in range(positions):
            near = slice(p * reads, (p + 1) * reads)
            preact = preact_buf[part % 2, near, :].astype(BF16)
            spread = spread_buf[part % 2, near, :].astype(BF16)
            sigma = pl.reciprocal(1.0 + jnp.exp(-preact), approx=True)
            values = preact * sigma
            slope = sigma + values * (1.0 - sigma)
            slope_buf[part, near, :] = spread * slope
            values_buf[part, near, :] = values
            pool = jnp.sum((spread * values).astype(F32), axis=0, keepdims=True)
            pool_out[p : p + 1, cols] = pool
            if (p + 1) % (positions // 2) == 0:
                side = (p + 1) // (positions // 2) - 1
                at = pl.ds(side * (positions // 2) * reads, positions // 2 * reads)
                pairs = ((slope_buf, slope_out), (values_buf, values_out))
                for k, (buf, out) in enumerate(pairs):
                    sem = sems.at[2 + 4 * part + 2 * side + k]
                    stores.append(pltpu.make_async_copy(buf.at[part, at], out.at[part, at], sem))
                    stores[-1].start()
    for store in stores:
        store.wait()


VMEM = pl.BlockSpec(memory_space=pltpu.VMEM)
SMEM = pl.BlockSpec(memory_space=pltpu.SMEM)
HBM = pl.BlockSpec(memory_space=pltpu.HBM)
ANY = pl.BlockSpec(memory_space=pl.ANY)


def in_hbm(*arrays):
    return [pltpu.with_memory_space_constraint(array, pltpu.HBM) for array in arrays]


def encode(depth_index, counts, feats, *rest):
    positions, reads, channels = feats.shape
    rows = positions * reads
    step = TILE * reads
    return pl.pallas_call(
        encode_kernel,
        in_specs=[SMEM, SMEM, HBM] + [VMEM] * 5,
        out_specs=[HBM] + [VMEM] * 3,
        out_shape=[
            pltpu.HBM((rows, channels), BF16),
            jax.ShapeDtypeStruct((rows, LANES), BF16),
            jax.ShapeDtypeStruct((positions, LANES), F32),
            jax.ShapeDtypeStruct((positions, LANES), BF16),
        ],
        scratch_shapes=[
            pltpu.VMEM(feats.shape, BF16),
            pltpu.VMEM((rows, channels), BF16),
            pltpu.VMEM((step, LANES), BF16),
            pltpu.VMEM((step, channels), F32),
            pltpu.VMEM((rows, LANES), F32),
            pltpu.VMEM((positions, LANES), F32),
            pltpu.SemaphoreType.DMA((positions // TILE,)),
            pltpu.SemaphoreType.DMA((positions // TILE,)),
        ],
        compiler_params=pltpu.CompilerParams(vmem_limit_bytes=20 * 2**20),
        cost_estimate=pl.CostEstimate(
            flops=2 * rows * channels * 256, bytes_accessed=4 * 2**20, transcendentals=rows * LANES
        ),
    )(depth_index, *in_hbm(counts, feats, *rest))


def make_values(features, pair, value_weight, positions):
    rows, channels = features.shape
    return pl.pallas_call(
        value_kernel,
        in_specs=[VMEM, VMEM, HBM],
        out_specs=[HBM] * 3 + [VMEM],
        out_shape=[
            pltpu.HBM((rows, LANES), BF16),
            pltpu.HBM((N_DEPTH, rows, OWN_UNITS), BF16),
            pltpu.HBM((N_DEPTH, rows, OWN_UNITS), BF16),
            jax.ShapeDtypeStruct((positions, UNITS), F32),
        ],
        scratch_shapes=[
            pltpu.VMEM((rows, channels), BF16),
            pltpu.VMEM((N_DEPTH, rows, OWN_UNITS), BF16),
            pltpu.VMEM((N_DEPTH, rows, OWN_UNITS), BF16),
            pltpu.VMEM((2, rows, OWN_UNITS), F32),
            pltpu.VMEM((2, rows, OWN_UNITS), F32),
            pltpu.SemaphoreType.DMA,
            pltpu.SemaphoreType.DMA((2 + 4 * N_DEPTH,)),
        ],
        compiler_params=pltpu.CompilerParams(vmem_limit_bytes=32 * 2**20),
        cost_estimate=pl.CostEstimate(
            flops=2 * rows * UNITS * (channels + 256),
            bytes_accessed=16 * 2**20,
            transcendentals=rows * UNITS,
        ),
    )(pair, value_weight, *in_hbm(features))


def rim_kernel(before_ref, local_ref, after_ref, weight_ref, stat_ref, payload_out, cols_out):
    positions, outs = local_ref.shape
    taps = weight_ref.shape[0]
    half = taps // 2
    rows = cols_out.shape[1]
    low = before_ref[positions - 16 :, :].astype(F32)[16 - half :]
    high = after_ref[0:16, :].astype(F32)[:half]
    local = local_ref[...].astype(F32)
    pad = jnp.zeros((rows - positions - 2 * half, outs), F32)
    rim = jnp.concatenate([low, local, high, pad], axis=0).astype(BF16)
    cols = jnp.concatenate([local, low, high, pad], axis=0).astype(BF16)
    grad = jnp.zeros((positions, OWN_UNITS), F32)
    for k in range(taps):
        first = 2 * half - k
        grad += dot(rim, weight_ref[k], 1, 1)[first : first + positions]
    for d in range(N_DEPTH):
        payload_out[d, :, 0:OWN_UNITS] = grad.astype(BF16)
        payload_out[d, :, OWN_UNITS:] = stat_ref[...]
    for i in range(cols_out.shape[0]):
        cols_out[i] = cols[:, i * 128 : (i + 1) * 128]


def joint_stats(payload_ref, top):
    positions = payload_ref.shape[1]
    lane = iota((LANES, LANES), 0)
    target = iota((LANES, LANES), 1)
    wanted = target < 2 * HEADS
    pick_top = (wanted & (lane < 16) & (lane % HEADS == target % HEADS)).astype(BF16)
    pick_total = wanted & (lane >= 16) & (lane < 32) & (lane % HEADS == target % HEADS)
    stats = [payload_ref[d, :, OWN_UNITS:] for d in range(N_DEPTH)]
    tops = [dot(stat, pick_top) for stat in stats]
    joint = jnp.maximum(jnp.maximum(tops[0], tops[1]), jnp.maximum(tops[2], tops[3]))
    total = jnp.zeros_like(joint)
    for d in range(N_DEPTH):
        total += jnp.exp(tops[d] - joint) * dot(stats[d], pick_total.astype(BF16))
    small = iota((positions, LANES), 1) < 2 * HEADS
    total = jnp.where(small, total, 1.0)
    return jnp.where(small, jnp.exp(jnp.where(small, top - joint, 0.0)) / total, 0.0)


def paired(value):
    high, low = split_pair(value)
    return jnp.where(iota(value.shape, 1) < HEADS, high, low).astype(BF16)


def spread_of(d):
    lanes = iota((LANES, OWN_UNITS), 0)
    head = iota((LANES, OWN_UNITS), 1) // WIDTH + d * OWN
    return ((lanes == head) | (lanes == head + HEADS)).astype(BF16)


def share_kernel(depth_ref, payload_ref, top_ref, pool_ref, cols_ref, send_out, scale_out):
    positions = top_ref.shape[0]
    quarter = positions // N_DEPTH
    scale = joint_stats(payload_ref, top_ref[...])
    scale_out[...] = scale
    pair = paired(scale)
    row = iota((OWN_UNITS, OWN_UNITS), 0)
    column = iota((OWN_UNITS, OWN_UNITS), 1)
    source = ((column % 128) // 8) * 16 + (column // 128) * 8 + column % 8
    order = (row == source).astype(BF16)
    lane = iota((positions, LANES), 1)
    totals = jnp.zeros((positions, LANES), F32)
    for d in range(N_DEPTH):
        part = pool_ref[:, d * OWN_UNITS : (d + 1) * OWN_UNITS] * dot(pair, spread_of(d))
        product = payload_ref[d, :, 0:OWN_UNITS].astype(F32) * part
        for i in range(OWN):
            span = slice(i * WIDTH, (i + 1) * WIDTH)
            total = jnp.sum(product[:, span], axis=1, keepdims=True)
            totals = jnp.where(lane == d * OWN + i, total, totals)
        part = dot(part.astype(BF16), order).astype(BF16)
        for peer in range(8):
            xlo = peer // 4
            send_out[8 * d + peer, 0:positions, :] = part[:, xlo * 128 : (xlo + 1) * 128]
    same = (iota((positions, LANES), 0) == iota((positions, LANES), 1)).astype(BF16)
    other = (iota((positions, LANES), 0) + positions == iota((positions, LANES), 1)).astype(BF16)
    high, low = split_pair(totals)
    turned = dot(high.astype(BF16), same, 0, 0) + dot(low.astype(BF16), other, 0, 0)
    extra = [turned[0:HEADS], None, jnp.zeros((4, LANES), F32)]
    own = pl.multiple_of(depth_ref[0] * quarter, quarter)
    for peer in range(4):
        rim = cols_ref[peer, positions : positions + 16, :].astype(F32)
        extra[1] = rim[0:4]
        rest = jnp.concatenate(extra, axis=0).astype(BF16)
        local = cols_ref[peer, pl.ds(own, quarter), :]
        for block in range(2 * N_DEPTH):
            index = 4 * block + peer
            send_out[index, positions : positions + quarter, :] = local
            send_out[index, positions + quarter :, :] = rest


def gradient_kernel(
    core_ref,
    payload_ref,
    scale_ref,
    features_hbm,
    slope_hbm,
    values_hbm,
    pair_hbm,
    mine_out,
    theirs_out,
    probs_hbm,
    total,
    slope_buf,
    values_buf,
    features_buf,
    grad_buf,
    scaled_buf,
    prob_buf,
    pair_buf,
    weights_buf,
    sems,
):
    positions = scale_ref.shape[0]
    rows = features_buf.shape[0]
    reads = rows // positions
    copies = [pltpu.make_async_copy(features_hbm, features_buf, sems.at[0])]
    for d in range(N_DEPTH):
        for k, (ref, buf) in enumerate(((slope_hbm, slope_buf), (values_hbm, values_buf))):
            copies.append(pltpu.make_async_copy(ref.at[d], buf.at[d], sems.at[1 + 2 * d + k]))
    copies.append(pltpu.make_async_copy(pair_hbm, pair_buf, sems.at[1 + 2 * N_DEPTH]))
    for i in [1, 0] + list(range(2, len(copies))):
        copies[i].start()
    pair = paired(scale_ref[...])
    first = core_ref[0] == 0

    def by_read(buf, p):
        shape = (16, OWN_UNITS)
        return jnp.broadcast_to(buf[p : p + 1, :], shape).astype(BF16)[None]

    split = (reads // 16, 16, OWN_UNITS)

    def multiply(buf, d, factor):
        for p in range(positions):
            span = slice(p * reads, (p + 1) * reads)
            term = buf[d, span, :].reshape(split) * by_read(factor, p)
            buf[d, span, :] = term.reshape(reads, OWN_UNITS)

    def set_factors(d):
        grad = payload_ref[d, :, 0:OWN_UNITS].astype(F32)
        grad_buf[d % 2] = grad
        scaled_buf[d % 2] = grad * dot(pair, spread_of(d))

    def pack(d):
        for peer in range(4 * d, 4 * d + 4):
            base = d * OWN_UNITS + (peer % 4) * 4
            for q in range(4):
                for t in range(2):
                    zero = total[q, pl.ds(base + t, N_Z, stride=16), :]
                    one = total[q, pl.ds(base + 2 + t, N_Z, stride=16), :]
                    span = slice(q * 32 + t * 16, q * 32 + t * 16 + 16)
                    mine_out[peer, span, :] = jnp.where(first, zero, one).astype(BF16)
                    theirs_out[peer, span, :] = jnp.where(first, one, zero).astype(BF16)

    set_factors(0)
    copies[1].wait()
    multiply(slope_buf, 0, scaled_buf.at[0])
    copies[0].wait()
    for d in range(N_DEPTH):
        cols = slice(d * OWN_UNITS, (d + 1) * OWN_UNITS)
        copies[2 + 2 * d].wait()
        if d + 1 < N_DEPTH:
            copies[3 + 2 * d].wait()
            set_factors(d + 1)
        term = dot(slope_buf[d], features_buf[...], 0, 0)
        for q in range(4):
            total[q, cols, :] = term[:, q * 128 : (q + 1) * 128]
        if d + 1 < N_DEPTH:
            multiply(slope_buf, d + 1, scaled_buf.at[(d + 1) % 2])
        multiply(values_buf, d, grad_buf.at[d % 2])
        if d:
            pack(d - 1)
        term = dot(values_buf[d], spread_of(d), 1, 1)
        if d == 0:
            prob_buf[...] = term
        else:
            prob_buf[...] += term
    copies[1 + 2 * N_DEPTH].wait()
    lane = iota((LANES, LANES), 0)
    target = iota((LANES, LANES), 1)
    both = (lane < 16) & (target < 16) & (lane % HEADS == target % HEADS)
    weights_buf[...] = dot(pair_buf[...], both.astype(BF16))
    lane = iota((reads, LANES), 1)
    for p in range(positions):
        span = slice(p * reads, (p + 1) * reads)
        probs = weights_buf[span, :] * scale_ref[p : p + 1, :]
        prob_buf[span, :] = jnp.where(lane < HEADS, probs * prob_buf[span, :], probs)
    store = pltpu.make_async_copy(prob_buf, probs_hbm, sems.at[2 + 2 * N_DEPTH])
    store.start()
    pack(N_DEPTH - 1)
    store.wait()


def gradients(core_index, payload, scale, features, *rest):
    rows, channels = features.shape
    positions = scale.shape[0]
    shape = (PLANE, 128, 128)
    return pl.pallas_call(
        gradient_kernel,
        in_specs=[SMEM] + [VMEM] * 2 + [HBM] * 4,
        out_specs=[VMEM, VMEM, HBM],
        out_shape=[
            jax.ShapeDtypeStruct(shape, BF16),
            jax.ShapeDtypeStruct(shape, BF16),
            pltpu.HBM((rows, LANES), F32),
        ],
        scratch_shapes=[
            pltpu.VMEM((4, UNITS + 16, 128), F32),
            pltpu.VMEM((N_DEPTH, rows, OWN_UNITS), BF16),
            pltpu.VMEM((N_DEPTH, rows, OWN_UNITS), BF16),
            pltpu.VMEM((rows, channels), BF16),
            pltpu.VMEM((2, positions, OWN_UNITS), F32),
            pltpu.VMEM((2, positions, OWN_UNITS), F32),
            pltpu.VMEM((rows, LANES), F32),
            pltpu.VMEM((rows, LANES), BF16),
            pltpu.VMEM((rows, LANES), F32),
            pltpu.SemaphoreType.DMA((3 + 2 * N_DEPTH,)),
        ],
        compiler_params=pltpu.CompilerParams(vmem_limit_bytes=36 * 2**20),
        cost_estimate=pl.CostEstimate(
            flops=2 * rows * UNITS * (channels + 256),
            bytes_accessed=16 * 2**20,
            transcendentals=10**4,
        ),
    )(core_index, payload, scale, *in_hbm(features, *rest))


def score_kernel(
    place_ref,
    recv_ref,
    probs_hbm,
    features_hbm,
    score_out,
    probs_buf,
    features_buf,
    score_buf,
    row_buf,
    sems,
):
    rows = probs_buf.shape[0]
    positions = recv_ref.shape[1] - 32
    reads = rows // positions
    load = [
        pltpu.make_async_copy(probs_hbm, probs_buf, sems.at[0]),
        pltpu.make_async_copy(features_hbm, features_buf, sems.at[1]),
    ]
    load[0].start()
    load[1].start()
    row = jnp.zeros((16, LANES), F32)
    for d in range(N_DEPTH):
        row += recv_ref[8 * d + place_ref[0], positions + 16 : positions + 32, :].astype(F32)
    high, low = split_pair(row)
    pick = iota((16, LANES), 0) == iota((16, LANES), 1)
    pick = (pick & (iota((16, LANES), 0) < HEADS)).astype(BF16)
    turned = dot(high.astype(BF16), pick, 0, 0) + dot(low.astype(BF16), pick, 0, 0)
    row_buf[...] = turned[0:positions] + turned[positions : 2 * positions]
    load[0].wait()
    for p in range(positions):
        span = slice(p * reads, (p + 1) * reads)
        term = probs_buf[span, :]
        probs = pltpu.roll(term, LANES - HEADS, 1)
        score_buf[span, :] = (term - probs * row_buf[p : p + 1, :]).astype(BF16)
    load[1].wait()
    score = dot(score_buf[...], features_buf[...], 0, 0)[0:HEADS]
    score = [score[:, q * 128 : (q + 1) * 128] for q in range(4)]
    score_out[...] = jnp.concatenate(score, axis=0).astype(BF16)


def scores(place, recv, probs, features):
    rows, channels = features.shape
    positions = recv.shape[1] - 32
    return pl.pallas_call(
        score_kernel,
        in_specs=[SMEM, VMEM, HBM, HBM],
        out_specs=VMEM,
        out_shape=jax.ShapeDtypeStruct((4 * HEADS, 128), BF16),
        scratch_shapes=[
            pltpu.VMEM((rows, LANES), F32),
            pltpu.VMEM((rows, channels), BF16),
            pltpu.VMEM((rows, LANES), BF16),
            pltpu.VMEM((positions, LANES), F32),
            pltpu.SemaphoreType.DMA((2,)),
        ],
        compiler_params=pltpu.CompilerParams(vmem_limit_bytes=16 * 2**20),
        cost_estimate=pl.CostEstimate(flops=10**8, bytes_accessed=10**6, transcendentals=0),
    )(place, recv, *in_hbm(probs, features))


def pair_kernel(mine_ref, theirs_ref, score_ref, other_ref, send_out):
    score = score_ref[...].astype(F32) + other_ref[...].astype(F32)
    score = score.astype(BF16)
    for peer in range(PLANE):
        value = mine_ref[peer].astype(F32) + theirs_ref[peer].astype(F32)
        send_out[peer, 0:128, :] = value.astype(BF16)
        send_out[peer, 128:160, :] = score


def conv_kernel(recv_ref, part_out):
    positions = recv_ref.shape[1] - 32
    taps = part_out.shape[1] // 8
    half = taps // 2
    left, grads = [], []
    for j in range(8):
        pooled = recv_ref[j, 0:positions, :].astype(F32)
        local = [recv_ref[j, positions : positions + 16, :]]
        for d in range(1, N_DEPTH):
            pooled += recv_ref[8 * d + j, 0:positions, :].astype(F32)
            local.append(recv_ref[8 * d + j, positions : positions + 16, :])
        left.append(pooled.astype(BF16))
        rest = recv_ref[j, positions + 16 : positions + 32, :].astype(F32)
        low, high = rest[8 : 8 + half], rest[8 + half : 8 + 2 * half]
        grads.append(jnp.concatenate([low] + [x.astype(F32) for x in local] + [high], axis=0))
    left = jnp.concatenate(left, axis=0)
    for k in range(taps):
        first = 2 * half - k
        shifted = jnp.concatenate([grad[first : first + positions] for grad in grads], axis=0)
        part = dot(left, shifted.astype(BF16), 0, 0)
        part_out[:, k * 8 : (k + 1) * 8, :] = part.reshape(N_Z, 8, 128)


def line_kernel(recv_ref, conv_ref, send_out, total):
    value = recv_ref[0].astype(F32)
    for peer in range(1, PLANE):
        value += recv_ref[peer].astype(F32)
    total[...] = value
    score = value[128:160]
    for z in range(N_Z):
        block = jnp.concatenate([total[pl.ds(z, 8, stride=16), :], score, conv_ref[z]], axis=0)
        send_out[z] = block.astype(BF16)


def last_kernel(recv_ref, value_out, score_out, conv_out):
    value = recv_ref[0].astype(F32)
    for z in range(1, N_Z):
        value += recv_ref[z].astype(F32)
    for q in range(4):
        span = slice(q * 128, (q + 1) * 128)
        value_out[:, span] = value[2 * q : 2 * q + 2]
        score_out[:, span] = value[8 + 8 * q : 16 + 8 * q]
    for k in range(conv_out.shape[0]):
        conv_out[k] = value[40 + 8 * k : 48 + 8 * k]


def small_call(kernel, shapes, *operands, specs=None, scratch=(), mib=6):
    single = not isinstance(shapes, list)
    return pl.pallas_call(
        kernel,
        in_specs=specs or [VMEM] * len(operands),
        out_specs=VMEM if single else [VMEM] * len(shapes),
        out_shape=shapes,
        scratch_shapes=list(scratch),
        compiler_params=pltpu.CompilerParams(vmem_limit_bytes=mib * 2**20),
        cost_estimate=pl.CostEstimate(flops=10**6, bytes_accessed=10**5, transcendentals=0),
    )(*operands)


def exchange(block, axis):
    return lax.ppermute(block, axis, [(0, 1), (1, 0)])


def body(
    read_feats,
    base_codes,
    qual_codes,
    depth_counts,
    base_table,
    qual_table,
    value_weight,
    score_weight,
    conv_weight,
    cotangent,
):
    _, positions, reads, channels = read_feats.shape
    block_units, taps, outs = conv_weight.shape
    depth_index = lax.axis_index("depth")
    core_index = lax.axis_index("core")
    def shaped(*shape, kind=BF16):
        return jax.ShapeDtypeStruct(shape, kind)

    count = lax.axis_size(SEQ)
    forward = [(i, i + 1) for i in range(count - 1)]
    grad_local = cotangent[0]
    before = lax.ppermute(grad_local, SEQ, forward)
    after = lax.ppermute(grad_local, SEQ, [(b, a) for a, b in forward])

    features, pair, top, stat = encode(
        depth_index.reshape(1),
        depth_counts[0],
        read_feats[0],
        base_codes[0].T,
        qual_codes[0].T,
        base_table,
        qual_table,
        score_weight.T,
    )

    payload, cols = small_call(
        rim_kernel,
        [shaped(N_DEPTH, positions, OWN_UNITS + LANES), shaped(4, RIM, 128)],
        before,
        grad_local,
        after,
        conv_weight.transpose(1, 0, 2),
        stat,
    )
    payload = lax.all_to_all(payload, "depth", split_axis=0, concat_axis=0, tiled=True)

    pair, slope, values, pool = make_values(features, pair, value_weight, positions)

    send, scale = small_call(
        share_kernel,
        [
            shaped(8 * N_DEPTH, positions + 32, 128),
            shaped(positions, LANES, kind=F32),
        ],
        depth_index.reshape(1),
        payload,
        top,
        pool,
        cols,
        specs=[SMEM] + [VMEM] * 4,
    )
    recv = lax.all_to_all(
        send, ("depth", "xlo", "xhi", "core"), split_axis=0, concat_axis=0, tiled=True
    )

    mine, theirs, probs = gradients(
        core_index.reshape(1), payload, scale, features, slope, values, pair
    )
    place = lax.axis_index(("xlo", "xhi", "core")).reshape(1)
    theirs = exchange(theirs, "core")
    score = scores(place, recv, probs, features)
    other = exchange(score, "core")
    plane_send = small_call(
        pair_kernel, shaped(PLANE, 160, 128), mine, theirs, score, other
    )
    plane_recv = lax.all_to_all(
        plane_send, ("depth", "xlo", "xhi"), split_axis=0, concat_axis=0, tiled=True
    )
    conv_part = small_call(conv_kernel, shaped(N_Z, 8 * taps, 128, kind=F32), recv)

    line_send = small_call(
        line_kernel,
        shaped(N_Z, 40 + 8 * taps, 128),
        plane_recv,
        conv_part,
        scratch=[pltpu.VMEM((160, 128), F32)],
    )
    line_recv = lax.all_to_all(line_send, "z", split_axis=0, concat_axis=0, tiled=True)
    value_weight_grad, score_weight_grad, conv_weight_grad = small_call(
        last_kernel,
        [
            shaped(2, channels, kind=F32),
            shaped(HEADS, channels, kind=F32),
            shaped(taps, 8, 128, kind=F32),
        ],
        line_recv,
    )
    return (value_weight_grad, score_weight_grad.T, conv_weight_grad.transpose(1, 0, 2))


def solution(mesh):
    fine = Mesh(mesh.devices.reshape(N_DEPTH, N_Z, 2, 2, 2), AXES)
    rep = ("xhi", "core")
    placed = (
        P(rep, SEQ, "depth", None),
        P(rep, SEQ, "depth"),
        P(rep, SEQ, "depth"),
        P(rep, SEQ),
        P(),
        P(),
        P(),
        P(),
        P("depth", None, None),
        P(rep, SEQ, None),
    )
    return jax.shard_map(
        body,
        mesh=fine,
        in_specs=placed,
        out_specs=(P(AXES, None), P(), P(("depth",) + SEQ, None, rep)),
        check_vma=False,
    )
```

```python
import jax
import jax.numpy as jnp
from jax import lax
from jax.experimental import pallas as pl
from jax.experimental.pallas import tpu as pltpu
from jax.sharding import Mesh, PartitionSpec as P

AXES = ("depth", "z", "xlo", "xhi", "core")
SEQ = ("z", "xlo")
F32 = jnp.float32
BF16 = jnp.bfloat16
I32 = jnp.int32

TILE = 16
LANES = 128
HEADS = 8
WIDTH = 128
OWN = 2
OWN_UNITS = OWN * WIDTH
UNITS = HEADS * WIDTH
RIM = 80
N_DEPTH = 4
N_Z = 16
PLANE = 16


def iota(shape, dim):
    return lax.broadcasted_iota(I32, shape, dim)


def dot(a, b, ca=1, cb=0):
    return lax.dot_general(a, b, (((ca,), (cb,)), ((), ())), preferred_element_type=F32)


def split_pair(value):
    high = value.astype(BF16).astype(F32)
    return high, value - high


def encode_kernel(
    depth_ref,
    count_ref,
    feat_hbm,
    conv_hbm,
    base_codes_ref,
    qual_codes_ref,
    base_ref,
    qual_ref,
    score_ref,
    features_out,
    pair_out,
    top_out,
    stat_out,
    conv_out,
    feat_buf,
    features_buf,
    hot_buf,
    embed_buf,
    score_buf,
    stat_buf,
    sems,
    out_sems,
):
    positions, reads, channels = feat_buf.shape
    tiles = positions // TILE
    rows = TILE * reads
    copies = []
    for i in range(tiles):
        span = pl.ds(i * TILE, TILE)
        copies.append(pltpu.make_async_copy(feat_hbm.at[span], feat_buf.at[span], sems.at[i]))
        copies[i].start()
    stores = []
    fetch = pltpu.make_async_copy(conv_hbm, conv_out, out_sems.at[tiles])
    n_qual, n_base = qual_ref.shape[0], base_ref.shape[0]
    place = (iota((LANES, n_qual), 0) == iota((LANES, n_qual), 1)).astype(BF16)
    table = dot(place, qual_ref[...])
    place = (iota((LANES, n_base), 0) == iota((LANES, n_base), 1) + 96).astype(BF16)
    table = (table + dot(place, base_ref[...])).astype(BF16)
    slot = iota((LANES, HEADS), 0)
    place = (slot % HEADS == iota((LANES, HEADS), 1)) & (slot < 4 * HEADS)
    score_weight = dot(place.astype(BF16), score_ref[...]).astype(BF16)
    lane = iota((reads, LANES), 1)
    read = iota((reads, LANES), 0) + depth_ref[0] * reads
    for i in range(tiles):
        first_row = i * rows
        for p in range(TILE):
            at = i * TILE + p
            qual = jnp.broadcast_to(qual_codes_ref[:, at : at + 1], (reads, LANES))
            base = jnp.broadcast_to(base_codes_ref[:, at : at + 1], (reads, LANES))
            hot = (lane == qual) | (lane == base + 96)
            hot_buf[p * reads : (p + 1) * reads, :] = hot.astype(BF16)
        embed_buf[...] = dot(hot_buf[...], table)
        copies[i].wait()
        if i == tiles - 1:
            fetch.start()
        for p in range(TILE):
            near = slice(p * reads, (p + 1) * reads)
            feature = feat_buf[i * TILE + p].astype(F32) + embed_buf[near, :]
            far = slice(first_row + p * reads, first_row + (p + 1) * reads)
            features_buf[far, :] = feature.astype(BF16)
        at = pl.ds(first_row, rows)
        stores.append(
            pltpu.make_async_copy(features_buf.at[at], features_out.at[at], out_sems.at[i])
        )
        stores[i].start()
    features = features_buf[...]
    score_buf[...] = dot(features, score_weight, 1, 1)
    for p in range(positions):
        near = slice(p * reads, (p + 1) * reads)
        scores = score_buf[near, :]
        live = read < count_ref[p]
        top = jnp.max(jnp.where(live, scores, -1e30), axis=0, keepdims=True)
        top_high, top_rest = split_pair(top)
        top_low = top_rest.astype(BF16).astype(F32)
        top = top_high + top_low
        weights = jnp.where(live, jnp.exp(scores - top), 0.0)
        total_high, total_low = split_pair(jnp.sum(weights, axis=0, keepdims=True))
        small = lane[0:1]
        stat_buf[p : p + 1, :] = jnp.where(
            small < 8,
            top_high,
            jnp.where(small < 16, top_low, jnp.where(small < 24, total_high, total_low)),
        )
        top_out[p : p + 1, :] = top
        high, low = split_pair(weights)
        pair_out[near, :] = jnp.where(lane < HEADS, high, low).astype(BF16)
    stat_out[...] = stat_buf[...].astype(BF16)
    for copy in stores + [fetch]:
        copy.wait()


def value_kernel(
    pair_ref,
    value_ref,
    features_hbm,
    pair_out,
    slope_out,
    values_out,
    pool_out,
    features_buf,
    slope_buf,
    values_buf,
    preact_buf,
    spread_buf,
    load_sem,
    sems,
):
    positions = pool_out.shape[0]
    reads = features_buf.shape[0] // positions
    load = pltpu.make_async_copy(features_hbm, features_buf, load_sem)
    load.start()
    spread_buf[0] = dot(pair_ref[...], spread_of(0))
    load.wait()
    stores = [pltpu.make_async_copy(pair_ref, pair_out, sems.at[1])]
    stores[0].start()

    def multiply(part):
        cols = slice(part * OWN_UNITS, (part + 1) * OWN_UNITS)
        preact_buf[part % 2] = dot(features_buf[...], value_ref[cols, :], 1, 1)
        if part:
            spread_buf[part % 2] = dot(pair_ref[...], spread_of(part))

    multiply(0)
    for part in range(N_DEPTH):
        if part + 1 < N_DEPTH:
            multiply(part + 1)
        cols = slice(part * OWN_UNITS, (part + 1) * OWN_UNITS)
        for p in range(positions):
            near = slice(p * reads, (p + 1) * reads)
            preact = preact_buf[part % 2, near, :].astype(BF16)
            spread = spread_buf[part % 2, near, :].astype(BF16)
            sigma = pl.reciprocal(1.0 + jnp.exp(-preact), approx=True)
            values = preact * sigma
            slope = sigma + values * (1.0 - sigma)
            slope_buf[part, near, :] = spread * slope
            values_buf[part, near, :] = values
            pool = jnp.sum((spread * values).astype(F32), axis=0, keepdims=True)
            pool_out[p : p + 1, cols] = pool
            if (p + 1) % (positions // 2) == 0:
                side = (p + 1) // (positions // 2) - 1
                at = pl.ds(side * (positions // 2) * reads, positions // 2 * reads)
                pairs = ((slope_buf, slope_out), (values_buf, values_out))
                for k, (buf, out) in enumerate(pairs):
                    sem = sems.at[2 + 4 * part + 2 * side + k]
                    stores.append(pltpu.make_async_copy(buf.at[part, at], out.at[part, at], sem))
                    stores[-1].start()
    for store in stores:
        store.wait()


VMEM = pl.BlockSpec(memory_space=pltpu.VMEM)
SMEM = pl.BlockSpec(memory_space=pltpu.SMEM)
HBM = pl.BlockSpec(memory_space=pltpu.HBM)
ANY = pl.BlockSpec(memory_space=pl.ANY)


def in_hbm(*arrays):
    return [pltpu.with_memory_space_constraint(array, pltpu.HBM) for array in arrays]


def encode(depth_index, counts, feats, conv, *rest):
    positions, reads, channels = feats.shape
    rows = positions * reads
    step = TILE * reads
    return pl.pallas_call(
        encode_kernel,
        in_specs=[SMEM, SMEM, HBM, HBM] + [VMEM] * 5,
        out_specs=[HBM] + [VMEM] * 4,
        out_shape=[
            pltpu.HBM((rows, channels), BF16),
            jax.ShapeDtypeStruct((rows, LANES), BF16),
            jax.ShapeDtypeStruct((positions, LANES), F32),
            jax.ShapeDtypeStruct((positions, LANES), BF16),
            jax.ShapeDtypeStruct(conv.shape, BF16),
        ],
        scratch_shapes=[
            pltpu.VMEM(feats.shape, BF16),
            pltpu.VMEM((rows, channels), BF16),
            pltpu.VMEM((step, LANES), BF16),
            pltpu.VMEM((step, channels), F32),
            pltpu.VMEM((rows, LANES), F32),
            pltpu.VMEM((positions, LANES), F32),
            pltpu.SemaphoreType.DMA((positions // TILE,)),
            pltpu.SemaphoreType.DMA((positions // TILE + 1,)),
        ],
        compiler_params=pltpu.CompilerParams(vmem_limit_bytes=20 * 2**20),
        cost_estimate=pl.CostEstimate(
            flops=2 * rows * channels * 256, bytes_accessed=4 * 2**20, transcendentals=rows * LANES
        ),
    )(depth_index, *in_hbm(counts, feats, conv, *rest))


def make_values(features, pair, value_weight, positions):
    rows, channels = features.shape
    return pl.pallas_call(
        value_kernel,
        in_specs=[VMEM, VMEM, HBM],
        out_specs=[HBM] * 3 + [VMEM],
        out_shape=[
            pltpu.HBM((rows, LANES), BF16),
            pltpu.HBM((N_DEPTH, rows, OWN_UNITS), BF16),
            pltpu.HBM((N_DEPTH, rows, OWN_UNITS), BF16),
            jax.ShapeDtypeStruct((positions, UNITS), F32),
        ],
        scratch_shapes=[
            pltpu.VMEM((rows, channels), BF16),
            pltpu.VMEM((N_DEPTH, rows, OWN_UNITS), BF16),
            pltpu.VMEM((N_DEPTH, rows, OWN_UNITS), BF16),
            pltpu.VMEM((2, rows, OWN_UNITS), F32),
            pltpu.VMEM((2, rows, OWN_UNITS), F32),
            pltpu.SemaphoreType.DMA,
            pltpu.SemaphoreType.DMA((2 + 4 * N_DEPTH,)),
        ],
        compiler_params=pltpu.CompilerParams(vmem_limit_bytes=32 * 2**20),
        cost_estimate=pl.CostEstimate(
            flops=2 * rows * UNITS * (channels + 256),
            bytes_accessed=16 * 2**20,
            transcendentals=rows * UNITS,
        ),
    )(pair, value_weight, *in_hbm(features))


def rim_kernel(before_ref, local_ref, after_ref, weight_ref, stat_ref, payload_out, cols_out):
    positions, outs = local_ref.shape
    taps = weight_ref.shape[0]
    half = taps // 2
    rows = cols_out.shape[1]
    low = before_ref[positions - 16 :, :].astype(F32)[16 - half :]
    high = after_ref[0:16, :].astype(F32)[:half]
    local = local_ref[...].astype(F32)
    pad = jnp.zeros((rows - positions - 2 * half, outs), F32)
    rim = jnp.concatenate([low, local, high, pad], axis=0).astype(BF16)
    cols = jnp.concatenate([local, low, high, pad], axis=0).astype(BF16)
    grad = jnp.zeros((positions, OWN_UNITS), F32)
    for k in range(taps):
        first = 2 * half - k
        grad += dot(rim, weight_ref[k], 1, 1)[first : first + positions]
    for d in range(N_DEPTH):
        payload_out[d, :, 0:OWN_UNITS] = grad.astype(BF16)
        payload_out[d, :, OWN_UNITS:] = stat_ref[...]
    for i in range(cols_out.shape[0]):
        cols_out[i] = cols[:, i * 128 : (i + 1) * 128]


def joint_stats(payload_ref, top):
    positions = payload_ref.shape[1]
    lane = iota((LANES, LANES), 0)
    target = iota((LANES, LANES), 1)
    wanted = target < 2 * HEADS
    pick_top = (wanted & (lane < 16) & (lane % HEADS == target % HEADS)).astype(BF16)
    pick_total = wanted & (lane >= 16) & (lane < 32) & (lane % HEADS == target % HEADS)
    stats = [payload_ref[d, :, OWN_UNITS:] for d in range(N_DEPTH)]
    tops = [dot(stat, pick_top) for stat in stats]
    joint = jnp.maximum(jnp.maximum(tops[0], tops[1]), jnp.maximum(tops[2], tops[3]))
    total = jnp.zeros_like(joint)
    for d in range(N_DEPTH):
        total += jnp.exp(tops[d] - joint) * dot(stats[d], pick_total.astype(BF16))
    small = iota((positions, LANES), 1) < 2 * HEADS
    total = jnp.where(small, total, 1.0)
    return jnp.where(small, jnp.exp(jnp.where(small, top - joint, 0.0)) / total, 0.0)


def paired(value):
    high, low = split_pair(value)
    return jnp.where(iota(value.shape, 1) < HEADS, high, low).astype(BF16)


def spread_of(d):
    lanes = iota((LANES, OWN_UNITS), 0)
    head = iota((LANES, OWN_UNITS), 1) // WIDTH + d * OWN
    return ((lanes == head) | (lanes == head + HEADS)).astype(BF16)


def share_kernel(depth_ref, payload_ref, top_ref, pool_ref, cols_ref, send_out, scale_out):
    positions = top_ref.shape[0]
    quarter = positions // N_DEPTH
    scale = joint_stats(payload_ref, top_ref[...])
    scale_out[...] = scale
    pair = paired(scale)
    row = iota((OWN_UNITS, OWN_UNITS), 0)
    column = iota((OWN_UNITS, OWN_UNITS), 1)
    source = ((column % 128) // 8) * 16 + (column // 128) * 8 + column % 8
    order = (row == source).astype(BF16)
    lane = iota((positions, LANES), 1)
    totals = jnp.zeros((positions, LANES), F32)
    for d in range(N_DEPTH):
        part = pool_ref[:, d * OWN_UNITS : (d + 1) * OWN_UNITS] * dot(pair, spread_of(d))
        product = payload_ref[d, :, 0:OWN_UNITS].astype(F32) * part
        for i in range(OWN):
            span = slice(i * WIDTH, (i + 1) * WIDTH)
            total = jnp.sum(product[:, span], axis=1, keepdims=True)
            totals = jnp.where(lane == d * OWN + i, total, totals)
        part = dot(part.astype(BF16), order).astype(BF16)
        for peer in range(8):
            xlo = peer // 4
            send_out[8 * d + peer, 0:positions, :] = part[:, xlo * 128 : (xlo + 1) * 128]
    same = (iota((positions, LANES), 0) == iota((positions, LANES), 1)).astype(BF16)
    other = (iota((positions, LANES), 0) + positions == iota((positions, LANES), 1)).astype(BF16)
    high, low = split_pair(totals)
    turned = dot(high.astype(BF16), same, 0, 0) + dot(low.astype(BF16), other, 0, 0)
    extra = [turned[0:HEADS], None, jnp.zeros((4, LANES), F32)]
    own = pl.multiple_of(depth_ref[0] * quarter, quarter)
    for peer in range(4):
        rim = cols_ref[peer, positions : positions + 16, :].astype(F32)
        extra[1] = rim[0:4]
        rest = jnp.concatenate(extra, axis=0).astype(BF16)
        local = cols_ref[peer, pl.ds(own, quarter), :]
        for block in range(2 * N_DEPTH):
            index = 4 * block + peer
            send_out[index, positions : positions + quarter, :] = local
            send_out[index, positions + quarter :, :] = rest


def gradient_kernel(
    core_ref,
    payload_ref,
    scale_ref,
    features_hbm,
    slope_hbm,
    values_hbm,
    pair_hbm,
    mine_out,
    theirs_out,
    probs_hbm,
    total,
    slope_buf,
    values_buf,
    features_buf,
    grad_buf,
    scaled_buf,
    prob_buf,
    pair_buf,
    weights_buf,
    sems,
):
    positions = scale_ref.shape[0]
    rows = features_buf.shape[0]
    reads = rows // positions
    copies = [pltpu.make_async_copy(features_hbm, features_buf, sems.at[0])]
    for d in range(N_DEPTH):
        for k, (ref, buf) in enumerate(((slope_hbm, slope_buf), (values_hbm, values_buf))):
            copies.append(pltpu.make_async_copy(ref.at[d], buf.at[d], sems.at[1 + 2 * d + k]))
    copies.append(pltpu.make_async_copy(pair_hbm, pair_buf, sems.at[1 + 2 * N_DEPTH]))
    for i in [1, 0] + list(range(2, len(copies))):
        copies[i].start()
    pair = paired(scale_ref[...])
    first = core_ref[0] == 0

    def by_read(buf, p):
        shape = (16, OWN_UNITS)
        return jnp.broadcast_to(buf[p : p + 1, :], shape).astype(BF16)[None]

    split = (reads // 16, 16, OWN_UNITS)

    def multiply(buf, d, factor):
        for p in range(positions):
            span = slice(p * reads, (p + 1) * reads)
            term = buf[d, span, :].reshape(split) * by_read(factor, p)
            buf[d, span, :] = term.reshape(reads, OWN_UNITS)

    def set_factors(d):
        grad = payload_ref[d, :, 0:OWN_UNITS].astype(F32)
        grad_buf[d % 2] = grad
        scaled_buf[d % 2] = grad * dot(pair, spread_of(d))

    def pack(d):
        for peer in range(4 * d, 4 * d + 4):
            base = d * OWN_UNITS + (peer % 4) * 4
            for q in range(4):
                for t in range(2):
                    zero = total[q, pl.ds(base + t, N_Z, stride=16), :]
                    one = total[q, pl.ds(base + 2 + t, N_Z, stride=16), :]
                    span = slice(q * 32 + t * 16, q * 32 + t * 16 + 16)
                    mine_out[peer, span, :] = jnp.where(first, zero, one).astype(BF16)
                    theirs_out[peer, span, :] = jnp.where(first, one, zero).astype(BF16)

    set_factors(0)
    copies[1].wait()
    multiply(slope_buf, 0, scaled_buf.at[0])
    copies[0].wait()
    for d in range(N_DEPTH):
        cols = slice(d * OWN_UNITS, (d + 1) * OWN_UNITS)
        copies[2 + 2 * d].wait()
        if d + 1 < N_DEPTH:
            copies[3 + 2 * d].wait()
            set_factors(d + 1)
        term = dot(slope_buf[d], features_buf[...], 0, 0)
        for q in range(4):
            total[q, cols, :] = term[:, q * 128 : (q + 1) * 128]
        if d + 1 < N_DEPTH:
            multiply(slope_buf, d + 1, scaled_buf.at[(d + 1) % 2])
        multiply(values_buf, d, grad_buf.at[d % 2])
        if d:
            pack(d - 1)
        term = dot(values_buf[d], spread_of(d), 1, 1)
        if d == 0:
            prob_buf[...] = term
        else:
            prob_buf[...] += term
    copies[1 + 2 * N_DEPTH].wait()
    lane = iota((LANES, LANES), 0)
    target = iota((LANES, LANES), 1)
    both = (lane < 16) & (target < 16) & (lane % HEADS == target % HEADS)
    weights_buf[...] = dot(pair_buf[...], both.astype(BF16))
    lane = iota((reads, LANES), 1)
    for p in range(positions):
        span = slice(p * reads, (p + 1) * reads)
        probs = weights_buf[span, :] * scale_ref[p : p + 1, :]
        prob_buf[span, :] = jnp.where(lane < HEADS, probs * prob_buf[span, :], probs)
    store = pltpu.make_async_copy(prob_buf, probs_hbm, sems.at[2 + 2 * N_DEPTH])
    store.start()
    pack(N_DEPTH - 1)
    store.wait()


def gradients(core_index, payload, scale, features, *rest):
    rows, channels = features.shape
    positions = scale.shape[0]
    shape = (PLANE, 128, 128)
    return pl.pallas_call(
        gradient_kernel,
        in_specs=[SMEM] + [VMEM] * 2 + [HBM] * 4,
        out_specs=[VMEM, VMEM, HBM],
        out_shape=[
            jax.ShapeDtypeStruct(shape, BF16),
            jax.ShapeDtypeStruct(shape, BF16),
            pltpu.HBM((rows, LANES), F32),
        ],
        scratch_shapes=[
            pltpu.VMEM((4, UNITS + 16, 128), F32),
            pltpu.VMEM((N_DEPTH, rows, OWN_UNITS), BF16),
            pltpu.VMEM((N_DEPTH, rows, OWN_UNITS), BF16),
            pltpu.VMEM((rows, channels), BF16),
            pltpu.VMEM((2, positions, OWN_UNITS), F32),
            pltpu.VMEM((2, positions, OWN_UNITS), F32),
            pltpu.VMEM((rows, LANES), F32),
            pltpu.VMEM((rows, LANES), BF16),
            pltpu.VMEM((rows, LANES), F32),
            pltpu.SemaphoreType.DMA((3 + 2 * N_DEPTH,)),
        ],
        compiler_params=pltpu.CompilerParams(vmem_limit_bytes=36 * 2**20),
        cost_estimate=pl.CostEstimate(
            flops=2 * rows * UNITS * (channels + 256),
            bytes_accessed=16 * 2**20,
            transcendentals=10**4,
        ),
    )(core_index, payload, scale, *in_hbm(features, *rest))


def score_kernel(
    place_ref,
    recv_ref,
    probs_hbm,
    features_hbm,
    score_out,
    probs_buf,
    features_buf,
    score_buf,
    row_buf,
    sems,
):
    rows = probs_buf.shape[0]
    positions = recv_ref.shape[1] - 32
    reads = rows // positions
    load = [
        pltpu.make_async_copy(probs_hbm, probs_buf, sems.at[0]),
        pltpu.make_async_copy(features_hbm, features_buf, sems.at[1]),
    ]
    load[0].start()
    load[1].start()
    row = jnp.zeros((16, LANES), F32)
    for d in range(N_DEPTH):
        row += recv_ref[8 * d + place_ref[0], positions + 16 : positions + 32, :].astype(F32)
    high, low = split_pair(row)
    pick = iota((16, LANES), 0) == iota((16, LANES), 1)
    pick = (pick & (iota((16, LANES), 0) < HEADS)).astype(BF16)
    turned = dot(high.astype(BF16), pick, 0, 0) + dot(low.astype(BF16), pick, 0, 0)
    row_buf[...] = turned[0:positions] + turned[positions : 2 * positions]
    load[0].wait()
    for p in range(positions):
        span = slice(p * reads, (p + 1) * reads)
        term = probs_buf[span, :]
        probs = pltpu.roll(term, LANES - HEADS, 1)
        score_buf[span, :] = (term - probs * row_buf[p : p + 1, :]).astype(BF16)
    load[1].wait()
    score = dot(score_buf[...], features_buf[...], 0, 0)[0:HEADS]
    score = [score[:, q * 128 : (q + 1) * 128] for q in range(4)]
    score_out[...] = jnp.concatenate(score, axis=0).astype(BF16)


def scores(place, recv, probs, features):
    rows, channels = features.shape
    positions = recv.shape[1] - 32
    return pl.pallas_call(
        score_kernel,
        in_specs=[SMEM, VMEM, HBM, HBM],
        out_specs=VMEM,
        out_shape=jax.ShapeDtypeStruct((4 * HEADS, 128), BF16),
        scratch_shapes=[
            pltpu.VMEM((rows, LANES), F32),
            pltpu.VMEM((rows, channels), BF16),
            pltpu.VMEM((rows, LANES), BF16),
            pltpu.VMEM((positions, LANES), F32),
            pltpu.SemaphoreType.DMA((2,)),
        ],
        compiler_params=pltpu.CompilerParams(vmem_limit_bytes=16 * 2**20),
        cost_estimate=pl.CostEstimate(flops=10**8, bytes_accessed=10**6, transcendentals=0),
    )(place, recv, *in_hbm(probs, features))


def pair_kernel(mine_ref, theirs_ref, score_ref, other_ref, send_out):
    score = score_ref[...].astype(F32) + other_ref[...].astype(F32)
    score = score.astype(BF16)
    for peer in range(PLANE):
        value = mine_ref[peer].astype(F32) + theirs_ref[peer].astype(F32)
        send_out[peer, 0:128, :] = value.astype(BF16)
        send_out[peer, 128:160, :] = score


def conv_kernel(recv_ref, part_out):
    positions = recv_ref.shape[1] - 32
    taps = part_out.shape[1] // 8
    half = taps // 2
    left, grads = [], []
    for j in range(8):
        pooled = recv_ref[j, 0:positions, :].astype(F32)
        local = [recv_ref[j, positions : positions + 16, :]]
        for d in range(1, N_DEPTH):
            pooled += recv_ref[8 * d + j, 0:positions, :].astype(F32)
            local.append(recv_ref[8 * d + j, positions : positions + 16, :])
        left.append(pooled.astype(BF16))
        rest = recv_ref[j, positions + 16 : positions + 32, :].astype(F32)
        low, high = rest[8 : 8 + half], rest[8 + half : 8 + 2 * half]
        grads.append(jnp.concatenate([low] + [x.astype(F32) for x in local] + [high], axis=0))
    left = jnp.concatenate(left, axis=0)
    for k in range(taps):
        first = 2 * half - k
        shifted = jnp.concatenate([grad[first : first + positions] for grad in grads], axis=0)
        part = dot(left, shifted.astype(BF16), 0, 0)
        part_out[:, k * 8 : (k + 1) * 8, :] = part.reshape(N_Z, 8, 128)


def line_kernel(recv_ref, conv_ref, send_out, total):
    value = recv_ref[0].astype(F32)
    for peer in range(1, PLANE):
        value += recv_ref[peer].astype(F32)
    total[...] = value
    score = value[128:160]
    for z in range(N_Z):
        block = jnp.concatenate([total[pl.ds(z, 8, stride=16), :], score, conv_ref[z]], axis=0)
        send_out[z] = block.astype(BF16)


def last_kernel(recv_ref, value_out, score_out, conv_out):
    value = recv_ref[0].astype(F32)
    for z in range(1, N_Z):
        value += recv_ref[z].astype(F32)
    for q in range(4):
        span = slice(q * 128, (q + 1) * 128)
        value_out[:, span] = value[2 * q : 2 * q + 2]
        score_out[:, span] = value[8 + 8 * q : 16 + 8 * q]
    for k in range(conv_out.shape[0]):
        conv_out[k] = value[40 + 8 * k : 48 + 8 * k]


def small_call(kernel, shapes, *operands, specs=None, scratch=(), mib=6):
    single = not isinstance(shapes, list)
    return pl.pallas_call(
        kernel,
        in_specs=specs or [VMEM] * len(operands),
        out_specs=VMEM if single else [VMEM] * len(shapes),
        out_shape=shapes,
        scratch_shapes=list(scratch),
        compiler_params=pltpu.CompilerParams(vmem_limit_bytes=mib * 2**20),
        cost_estimate=pl.CostEstimate(flops=10**6, bytes_accessed=10**5, transcendentals=0),
    )(*operands)


def exchange(block, axis):
    return lax.ppermute(block, axis, [(0, 1), (1, 0)])


def body(
    read_feats,
    base_codes,
    qual_codes,
    depth_counts,
    base_table,
    qual_table,
    value_weight,
    score_weight,
    conv_weight,
    cotangent,
):
    _, positions, reads, channels = read_feats.shape
    block_units, taps, outs = conv_weight.shape
    depth_index = lax.axis_index("depth")
    core_index = lax.axis_index("core")
    def shaped(*shape, kind=BF16):
        return jax.ShapeDtypeStruct(shape, kind)

    count = lax.axis_size(SEQ)
    forward = [(i, i + 1) for i in range(count - 1)]
    grad_local = cotangent[0]
    before = lax.ppermute(grad_local, SEQ, forward)
    after = lax.ppermute(grad_local, SEQ, [(b, a) for a, b in forward])

    features, pair, top, stat, conv_taps = encode(
        depth_index.reshape(1),
        depth_counts[0],
        read_feats[0],
        conv_weight.transpose(1, 0, 2),
        base_codes[0].T,
        qual_codes[0].T,
        base_table,
        qual_table,
        score_weight.T,
    )

    payload, cols = small_call(
        rim_kernel,
        [shaped(N_DEPTH, positions, OWN_UNITS + LANES), shaped(4, RIM, 128)],
        before,
        grad_local,
        after,
        conv_taps,
        stat,
    )
    payload = lax.all_to_all(payload, "depth", split_axis=0, concat_axis=0, tiled=True)

    pair, slope, values, pool = make_values(features, pair, value_weight, positions)

    send, scale = small_call(
        share_kernel,
        [
            shaped(8 * N_DEPTH, positions + 32, 128),
            shaped(positions, LANES, kind=F32),
        ],
        depth_index.reshape(1),
        payload,
        top,
        pool,
        cols,
        specs=[SMEM] + [VMEM] * 4,
    )
    recv = lax.all_to_all(
        send, ("depth", "xlo", "xhi", "core"), split_axis=0, concat_axis=0, tiled=True
    )

    mine, theirs, probs = gradients(
        core_index.reshape(1), payload, scale, features, slope, values, pair
    )
    place = lax.axis_index(("xlo", "xhi", "core")).reshape(1)
    theirs = exchange(theirs, "core")
    score = scores(place, recv, probs, features)
    other = exchange(score, "core")
    plane_send = small_call(
        pair_kernel, shaped(PLANE, 160, 128), mine, theirs, score, other
    )
    plane_recv = lax.all_to_all(
        plane_send, ("depth", "xlo", "xhi"), split_axis=0, concat_axis=0, tiled=True
    )
    conv_part = small_call(conv_kernel, shaped(N_Z, 8 * taps, 128, kind=F32), recv)

    line_send = small_call(
        line_kernel,
        shaped(N_Z, 40 + 8 * taps, 128),
        plane_recv,
        conv_part,
        scratch=[pltpu.VMEM((160, 128), F32)],
    )
    line_recv = lax.all_to_all(line_send, "z", split_axis=0, concat_axis=0, tiled=True)
    value_weight_grad, score_weight_grad, conv_weight_grad = small_call(
        last_kernel,
        [
            shaped(2, channels, kind=F32),
            shaped(HEADS, channels, kind=F32),
            shaped(taps, 8, 128, kind=F32),
        ],
        line_recv,
    )
    return (value_weight_grad, score_weight_grad.T, conv_weight_grad.transpose(1, 0, 2))


def solution(mesh):
    fine = Mesh(mesh.devices.reshape(N_DEPTH, N_Z, 2, 2, 2), AXES)
    rep = ("xhi", "core")
    placed = (
        P(rep, SEQ, "depth", None),
        P(rep, SEQ, "depth"),
        P(rep, SEQ, "depth"),
        P(rep, SEQ),
        P(),
        P(),
        P(),
        P(),
        P("depth", None, None),
        P(rep, SEQ, None),
    )
    return jax.shard_map(
        body,
        mesh=fine,
        in_specs=placed,
        out_specs=(P(AXES, None), P(), P(("depth",) + SEQ, None, rep)),
        check_vma=False,
    )
```
